32 devices in a mesh: tm: 4 (over y, x), rows: 8 (over z, core).
Axes of the slice: x: 2, y: 2, z: 4, core: 2. Of those that a mesh axis runs over, the one named last changes fastest.
Arguments:
- heights: bfloat16 [128, 1024, 1024], P('tm', 'rows'), may hold values from -6 to 6
Outputs:
- spectrum: float32 [64, 1024, 1024], P(None, ('tm', 'rows'))
The draws below stay inside these ranges and needn't reach their ends.
All inputs are finite; a program needn't handle non-finite values.
Results may differ from the reference program's by a relative error of at most 0.0035.
Values may be sent and summed in bfloat16 or wider, within the bound.
No kernel may reach another device: no remote copies, remote signals or barrier semaphores. Data moves between devices by JAX's collectives and lax.ppermute only.
A program may use at most 128 MiB of HBM per device.

```python
import math
import jax
import jax.numpy as jnp
from jax import lax

GRID = 1024
WIN = 64
FRAMES = 128


def level_of(stream_key, shape, cuts, smallest, largest):
    def one(axis_at, blocks):
        draws = jax.random.uniform(jax.random.fold_in(jax.random.fold_in(stream_key, 6), axis_at), (blocks,), jnp.float32, smallest / len(cuts), largest / len(cuts))
        return jnp.repeat(jnp.exp(draws), shape[axis_at] // blocks).reshape((-1,) + (1,) * (len(shape) - axis_at - 1))

    level = one(*cuts[0])
    for cut in cuts[1:]:
        level = level * one(*cut)
    return level


def centred(key, shape, width, reach, pieces=(), kind=jnp.bfloat16):
    factor_of = level_of(key, shape, pieces, -0.22, 0.18) if pieces else 1.0
    drawn = jax.random.normal(key, shape, jnp.float32) * width * factor_of
    return jnp.minimum(jnp.maximum(drawn, -reach), reach).astype(kind)


def setup_inputs(seed: int = 0) -> dict:
    streams_of = jax.random.split(jax.random.key(seed), 2)
    return {
        "heights": centred(streams_of[0], (FRAMES, GRID, GRID), 1.0, 6.0, ((0, 4), (1, 8))),
    }


def spatial_table(length):
    column = jnp.arange(2 * length, dtype=jnp.int32)
    column_part = column % 2
    wavenumber = column // 2
    position = jnp.arange(length, dtype=jnp.int32)
    angles = (position[:, None] * wavenumber[None, :] % length).astype(jnp.float32) * (2.0 * math.pi / length)
    values = jnp.where(column_part[None, :] == 0, jnp.cos(angles), -jnp.sin(angles))
    return (values / math.sqrt(length)).astype(jnp.bfloat16)

def make_column_table(length):
    position = jnp.arange(length, dtype=jnp.int32)
    angles = (position[:, None] * position[None, :] % length).astype(jnp.float32) * (2.0 * math.pi / length)
    values = jnp.concatenate([jnp.cos(angles), jnp.sin(angles)], 1)
    return (values / math.sqrt(length)).astype(jnp.bfloat16)

def time_table(window_len):
    time_step = jnp.arange(window_len, dtype=jnp.int32)
    hann_taper = 0.5 - 0.5 * jnp.cos(time_step.astype(jnp.float32) * (2.0 * math.pi / window_len))
    angles = (time_step[:, None] * time_step[None, :] % window_len).astype(jnp.float32) * (2.0 * math.pi / window_len)
    tables = jnp.stack([jnp.cos(angles) * hann_taper[None, :], jnp.sin(angles) * hann_taper[None, :]], 0)
    return (tables.astype(jnp.bfloat16), jnp.sum(hann_taper * hann_taper))

def window_power(window, time_taper):
    number = window.shape[2]
    length = window.shape[3]
    block_size = math.gcd(number, 64)

    def one_block(block_index, accumulated):
        slab_piece = lax.dynamic_slice_in_dim(window, block_index * block_size, block_size, 2)
        product = jnp.einsum('swt,tpqx->swpqx', time_taper.astype(jnp.float32), slab_piece.astype(jnp.float32))
        real_part = product[0, :, 0] + product[1, :, 1]
        imag_part = product[0, :, 1] - product[1, :, 0]
        return lax.dynamic_update_slice_in_dim(accumulated, real_part * real_part + imag_part * imag_part, block_index * block_size, 1)
    start = jnp.zeros((time_taper.shape[1], number, length), jnp.float32)
    return lax.fori_loop(0, number // block_size, one_block, start)

def reference(heights):
    number = heights.shape[0]
    length = heights.shape[1]
    row_table = spatial_table(length).astype(jnp.float32)
    col_table = make_column_table(length).astype(jnp.float32)
    time_taper, energy = time_table(WIN)
    hop_size = WIN // 2

    def frame_modes(single_frame):
        mixed_rows = jnp.dot(single_frame.astype(jnp.float32), row_table, preferred_element_type=jnp.float32).astype(jnp.bfloat16)
        product = jnp.dot(mixed_rows.T.astype(jnp.float32), col_table, preferred_element_type=jnp.float32)
        product = product.reshape(length, 2, 2, length)
        real_part = product[:, 0, 0] + product[:, 1, 1]
        imag_part = product[:, 1, 0] - product[:, 0, 1]
        return jnp.stack([real_part, imag_part], 0).astype(jnp.bfloat16)

    def block_modes(block_index):
        frame_block = lax.dynamic_slice_in_dim(heights, block_index * hop_size, hop_size, 0)
        return lax.map(frame_modes, frame_block)
    first_block = block_modes(jnp.int32(0))

    def advance(state_pair, block_index):
        previous, summed = state_pair
        current = block_modes(block_index)
        summed = summed + window_power(jnp.concatenate([previous, current], 0), time_taper)
        return ((current, summed), None)
    start = jnp.zeros((WIN, length, length), jnp.float32)
    (last_block, summed), unused = lax.scan(advance, (first_block, start), jnp.arange(1, number // hop_size, dtype=jnp.int32))
    return summed / ((number // hop_size - 1) * energy)
```

```python
import functools
import math

import jax
import jax.numpy as jnp
import ml_dtypes
import numpy as np
from jax import lax
from jax.experimental import pallas as pl
from jax.experimental.pallas import tpu as pltpu
from jax.sharding import PartitionSpec as P

AXES = ("tm", "rows")
LANES = 128
TILE = 8
VMEM_BYTES = 56 * 1024 * 1024


def to_bf16(values):
    return values.astype(ml_dtypes.bfloat16)


def unit_angles(left, right, modulus):
    return (np.outer(left, right) % modulus).astype(np.float32) * np.float32(2.0 * math.pi / modulus)


def y_table(length, wavenumbers):
    angles = unit_angles(wavenumbers, np.arange(length), length)
    pairs = np.stack([np.cos(angles), -np.sin(angles)], 1) / np.float32(math.sqrt(length))
    return to_bf16(pairs.reshape(2 * len(wavenumbers), length))


def x_table(length):
    angles = unit_angles(np.arange(length), np.arange(length), length)
    return to_bf16(
        np.concatenate([np.cos(angles), np.sin(angles)], 1) / np.float32(math.sqrt(length))
    )


def window_table(hop, windows):
    size = 2 * hop
    steps = np.arange(size)
    hann = np.float32(0.5) - np.float32(0.5) * np.cos(
        steps.astype(np.float32) * np.float32(2.0 * math.pi / size)
    )
    angles = unit_angles(steps, steps, size)
    cosine = to_bf16(np.cos(angles) * hann[None, :])
    sine = to_bf16(np.sin(angles) * hann[None, :])
    frames = hop * (windows + 1)
    table = np.zeros((windows, 2, size, 2, frames), ml_dtypes.bfloat16)
    for window in range(windows):
        at = slice(window * hop, window * hop + size)
        table[window, 0, :, 0, at] = cosine
        table[window, 0, :, 1, at] = sine
        table[window, 1, :, 1, at] = cosine
        table[window, 1, :, 0, at] = -sine
    return table.reshape(windows * 2 * size, 2 * frames), float(np.sum(hann * hann))


def reversal(size):
    matrix = np.zeros((size, size), ml_dtypes.bfloat16)
    matrix[np.arange(size), (size - np.arange(size)) % size] = 1
    return matrix


def row_transform_kernel(table_ref, heights_ref, out_ref, scratch):
    frames, rows, length = heights_ref.shape
    for frame in range(0, frames, 2):
        pair = heights_ref[frame : frame + 2].reshape(2 * rows, length)
        product = lax.dot_general(
            table_ref[...], pair, (((1,), (1,)), ((), ())), preferred_element_type=jnp.float32
        )
        scratch[:, frame, :] = product[:, :rows]
        scratch[:, frame + 1, :] = product[:, rows:]
    out_ref[...] = scratch[...].astype(jnp.bfloat16)


def row_transform(heights, table):
    frames, rows, length = heights.shape
    columns = table.shape[0]
    if rows != LANES:
        return jnp.einsum(
            "cy,fxy->cfx", table, heights, preferred_element_type=jnp.float32
        ).astype(jnp.bfloat16)
    step = 16
    return pl.pallas_call(
        row_transform_kernel,
        out_shape=jax.ShapeDtypeStruct((columns, frames, rows), jnp.bfloat16),
        grid=(frames // step,),
        in_specs=[
            pl.BlockSpec((columns, length), lambda i: (0, 0)),
            pl.BlockSpec((step, rows, length), lambda i: (i, 0, 0)),
        ],
        out_specs=pl.BlockSpec((columns, step, rows), lambda i: (0, i, 0)),
        scratch_shapes=[pltpu.VMEM((columns, step, rows), jnp.float32)],
        compiler_params=pltpu.CompilerParams(vmem_limit_bytes=VMEM_BYTES),
        cost_estimate=pl.CostEstimate(
            flops=2 * columns * frames * rows * length,
            bytes_accessed=2 * (heights.size + columns * length + columns * frames * rows),
            transcendentals=0,
        ),
        name="row_transform",
    )(table, heights)


def spectrum_kernel(scale, mirrored, *refs):
    if mirrored:
        pieces_ref, x_ref, window_ref, flip_w_ref, flip_k_ref, own_ref, mirror_ref, scratch = refs
    else:
        pieces_ref, x_ref, window_ref, own_ref = refs
    blocks, width, _, part, frames, rows = pieces_ref.shape
    length = x_ref.shape[0]
    all_frames = blocks * frames
    size = 2 * frames
    field = jnp.concatenate(
        [
            jnp.concatenate([pieces_ref[t, s, 0, p] for s in range(width)], 1)
            for p in range(part)
            for t in range(blocks)
        ],
        0,
    )
    chunk = math.gcd(length, 256)
    for at in range(0, length, chunk):
        cosine = jnp.dot(field, x_ref[:, at : at + chunk], preferred_element_type=jnp.float32)
        sine = jnp.dot(
            field, x_ref[:, length + at : length + at + chunk], preferred_element_type=jnp.float32
        )
        real_part = cosine[:all_frames] + sine[all_frames:]
        imag_part = cosine[all_frames:] - sine[:all_frames]
        modes = jnp.concatenate([real_part, imag_part], 0).astype(jnp.bfloat16)
        moved = jnp.dot(window_ref[...], modes, preferred_element_type=jnp.float32)
        power = moved * moved
        total = power[:size]
        for row in range(size, power.shape[0], size):
            total = total + power[row : row + size]
        total = total * scale
        own_ref[0, :, at : at + chunk] = total
        if mirrored:
            flipped = jnp.dot(
                flip_w_ref[...], total.astype(jnp.bfloat16), preferred_element_type=jnp.float32
            )
            row = pl.num_programs(0) - 1 - pl.program_id(0)
            scratch[row, :, at : at + chunk] = flipped.astype(jnp.bfloat16)
    if mirrored:

        @pl.when(pl.program_id(0) == pl.num_programs(0) - 1)
        def reverse():
            number = scratch.shape[0]
            flat = scratch[...].reshape(number * size, length)
            turned = jnp.dot(flat, flip_k_ref[...], preferred_element_type=jnp.float32)
            mirror_ref[...] = turned.astype(jnp.bfloat16).reshape(number, size, length)


def spectrum(pieces, tables, scale, mirrored):
    blocks, width, number, part, frames, rows = pieces.shape
    length = width * rows
    size = 2 * frames
    if rows != LANES:
        pieces = pieces.transpose(0, 2, 3, 4, 1, 5).reshape(blocks, 1, number, part, frames, length)
        width, rows = 1, length
    x_values, windows, flip_w, flip_k = tables
    whole = lambda array: pl.BlockSpec(array.shape, lambda i: (0,) * array.ndim)
    operands = [pieces, x_values, windows]
    in_specs = [
        pl.BlockSpec((blocks, width, 1, part, frames, rows), lambda i: (0, 0, i, 0, 0, 0)),
        whole(x_values),
        whole(windows),
    ]
    out_shape = [jax.ShapeDtypeStruct((number, size, length), jnp.float32)]
    out_specs = [pl.BlockSpec((1, size, length), lambda i: (i, 0, 0))]
    scratch_shapes = []
    if mirrored:
        operands += [flip_w, flip_k]
        in_specs += [whole(flip_w), whole(flip_k)]
        out_shape.append(jax.ShapeDtypeStruct((number, size, length), jnp.bfloat16))
        out_specs.append(pl.BlockSpec((number, size, length), lambda i: (0, 0, 0)))
        scratch_shapes.append(pltpu.VMEM((number, size, length), jnp.bfloat16))
    return pl.pallas_call(
        functools.partial(spectrum_kernel, scale, mirrored),
        out_shape=out_shape,
        grid=(number,),
        in_specs=in_specs,
        out_specs=out_specs,
        scratch_shapes=scratch_shapes,
        compiler_params=pltpu.CompilerParams(vmem_limit_bytes=VMEM_BYTES),
        cost_estimate=pl.CostEstimate(
            flops=number * 2 * length * (4 * blocks * frames * length + windows.size),
            bytes_accessed=2 * pieces.size + 6 * number * size * length,
            transcendentals=0,
        ),
        name="spectrum",
    )(*operands)


def turned(planes):
    return jnp.swapaxes(jnp.stack([plane.astype(jnp.float32) for plane in planes], 0), 0, 1)


def first_rows_kernel(high_ref, low_ref, edge_ref, mirror_ref, out_ref):
    octet = low_ref.shape[0] + 1
    out_ref[:, :octet] = turned([edge_ref[0]] + [low_ref[i] for i in range(octet - 1)])
    out_ref[:, octet : 2 * octet] = turned([high_ref[i] for i in range(octet)])
    out_ref[:, 2 * octet :] = turned([edge_ref[1]] + [mirror_ref[i] for i in range(octet - 1)])


def last_rows_kernel(given_ref, high_ref, low_ref, out_ref):
    del given_ref
    octet = low_ref.shape[0] + 1
    out_ref[...] = turned([high_ref[0]] + [low_ref[i] for i in range(octet - 1)])


def assemble(high, low, edge, high_mirror, low_mirror):
    octet, size, length = high.shape
    if octet % TILE:
        planes = [edge[:1], low, high, edge[1:], high_mirror, low_mirror]
        return jnp.concatenate([plane.astype(jnp.float32) for plane in planes], 0).transpose(1, 0, 2)
    step = 16
    over = lambda count: pl.BlockSpec((count, step, length), lambda i: (0, i, 0))
    out_shape = jax.ShapeDtypeStruct((size, 4 * octet, length), jnp.float32)
    params = pltpu.CompilerParams(vmem_limit_bytes=VMEM_BYTES)
    first = pl.pallas_call(
        first_rows_kernel,
        out_shape=out_shape,
        grid=(size // step,),
        in_specs=[over(octet), over(octet - 1), over(2), over(octet)],
        out_specs=pl.BlockSpec((step, 3 * octet, length), lambda i: (i, 0, 0)),
        compiler_params=params,
        name="first_rows",
    )(high, low, edge, high_mirror)
    return pl.pallas_call(
        last_rows_kernel,
        out_shape=out_shape,
        grid=(size // step,),
        in_specs=[
            pl.BlockSpec(memory_space=pl.ANY),
            pl.BlockSpec((1, step, length), lambda i: (octet - 1, i, 0)),
            over(octet - 1),
        ],
        out_specs=pl.BlockSpec((step, octet, length), lambda i: (i, 3, 0)),
        input_output_aliases={0: 0},
        compiler_params=params,
        name="last_rows",
    )(first, high_mirror, low_mirror)


def body(heights):
    frames, rows_dev, length = heights.shape
    tm_count = lax.axis_size("tm")
    rows_count = lax.axis_size("rows")
    devices = tm_count * rows_count
    owned = length // devices
    half = owned // 2
    windows, energy = window_table(frames, tm_count - 1)
    scale = 1.0 / ((tm_count - 1) * energy)
    tables = (x_table(length), windows, reversal(2 * frames), reversal(length))
    tables = tuple(jnp.asarray(table) for table in tables)
    opposite = [(device, devices - 1 - device) for device in range(devices)]

    def arrive(slots):
        wavenumbers = (np.arange(devices)[:, None] * owned + np.asarray(slots)[None, :]).reshape(-1)
        mixed = row_transform(heights, jnp.asarray(y_table(length, wavenumbers)))
        mixed = mixed.reshape(devices, len(slots), 2, frames, rows_dev)
        got = lax.all_to_all(mixed, AXES, split_axis=0, concat_axis=0, tiled=True)
        return got.reshape(tm_count, rows_count, len(slots), 2, frames, rows_dev)

    high_pieces = arrive(range(half // 2, half))
    low_pieces = arrive(range(1, half // 2))
    edge_pieces = arrive([0, half])
    high, high_mirror = spectrum(high_pieces, tables, scale, True)
    high_mirror = lax.ppermute(high_mirror, AXES, opposite)
    low, low_mirror = spectrum(low_pieces, tables, scale, True)
    low_mirror = lax.ppermute(low_mirror, AXES, opposite)
    (edge,) = spectrum(edge_pieces, tables, scale, False)
    return assemble(high, low, edge, high_mirror, low_mirror)


def solution(mesh):
    in_specs = (P("tm", "rows", None),)
    out_specs = P(None, ("tm", "rows"), None)
    return jax.shard_map(body, mesh=mesh, in_specs=in_specs, out_specs=out_specs, check_vma=False)
```

```python
import functools
import math

import jax
import jax.numpy as jnp
import ml_dtypes
import numpy as np
from jax import lax
from jax.experimental import pallas as pl
from jax.experimental.pallas import tpu as pltpu
from jax.sharding import PartitionSpec as P

AXES = ("tm", "rows")
LANES = 128
TILE = 8
SHARES = (4, 10, 15)
SMALL = pl.CostEstimate(flops=1 << 20, bytes_accessed=1 << 20, transcendentals=0)
LARGE = pl.CostEstimate(flops=1 << 40, bytes_accessed=1 << 20, transcendentals=0)
VMEM_BYTES = 56 * 1024 * 1024


def to_bf16(values):
    return values.astype(ml_dtypes.bfloat16)


def unit_angles(left, right, modulus):
    return (np.outer(left, right) % modulus).astype(np.float32) * np.float32(2.0 * math.pi / modulus)


def y_table(length, wavenumbers):
    angles = unit_angles(wavenumbers, np.arange(length), length)
    pairs = np.stack([np.cos(angles), -np.sin(angles)], 1) / np.float32(math.sqrt(length))
    return to_bf16(pairs.reshape(2 * len(wavenumbers), length))


def x_table(length):
    angles = unit_angles(np.arange(length), np.arange(length), length)
    return to_bf16(
        np.concatenate([np.cos(angles), np.sin(angles)], 1) / np.float32(math.sqrt(length))
    )


def window_table(hop, windows):
    size = 2 * hop
    steps = np.arange(size)
    hann = np.float32(0.5) - np.float32(0.5) * np.cos(
        steps.astype(np.float32) * np.float32(2.0 * math.pi / size)
    )
    angles = unit_angles(steps, steps, size)
    cosine = to_bf16(np.cos(angles) * hann[None, :])
    sine = to_bf16(np.sin(angles) * hann[None, :])
    frames = hop * (windows + 1)
    table = np.zeros((windows, 2, size, 2, frames), ml_dtypes.bfloat16)
    for window in range(windows):
        at = slice(window * hop, window * hop + size)
        table[window, 0, :, 0, at] = cosine
        table[window, 0, :, 1, at] = sine
        table[window, 1, :, 1, at] = cosine
        table[window, 1, :, 0, at] = -sine
    return table.reshape(windows * 2 * size, 2 * frames), float(np.sum(hann * hann))


def reversal(size):
    matrix = np.zeros((size, size), ml_dtypes.bfloat16)
    matrix[np.arange(size), (size - np.arange(size)) % size] = 1
    return matrix


def row_transform_kernel(table_ref, heights_ref, out_ref, scratch):
    frames, rows, length = heights_ref.shape
    for frame in range(0, frames, 2):
        pair = heights_ref[frame : frame + 2].reshape(2 * rows, length)
        product = lax.dot_general(
            table_ref[...], pair, (((1,), (1,)), ((), ())), preferred_element_type=jnp.float32
        )
        scratch[:, frame, :] = product[:, :rows]
        scratch[:, frame + 1, :] = product[:, rows:]
    out_ref[...] = scratch[...].astype(jnp.bfloat16)


def row_transform(heights, table):
    frames, rows, length = heights.shape
    columns = table.shape[0]
    if rows != LANES:
        return jnp.einsum(
            "cy,fxy->cfx", table, heights, preferred_element_type=jnp.float32
        ).astype(jnp.bfloat16)
    step = 16
    return pl.pallas_call(
        row_transform_kernel,
        out_shape=jax.ShapeDtypeStruct((columns, frames, rows), jnp.bfloat16),
        grid=(frames // step,),
        in_specs=[
            pl.BlockSpec((columns, length), lambda i: (0, 0)),
            pl.BlockSpec((step, rows, length), lambda i: (i, 0, 0)),
        ],
        out_specs=pl.BlockSpec((columns, step, rows), lambda i: (0, i, 0)),
        scratch_shapes=[pltpu.VMEM((columns, step, rows), jnp.float32)],
        compiler_params=pltpu.CompilerParams(vmem_limit_bytes=VMEM_BYTES),
        cost_estimate=SMALL,
        name="row_transform",
    )(table, heights)


def spectrum_kernel(scale, mirrored, *refs):
    if mirrored:
        pieces_ref, x_ref, window_ref, flip_w_ref, flip_k_ref, own_ref, mirror_ref, scratch = refs
    else:
        pieces_ref, x_ref, window_ref, own_ref = refs
    blocks, width, _, part, frames, rows = pieces_ref.shape
    length = x_ref.shape[0]
    all_frames = blocks * frames
    size = 2 * frames
    field = jnp.concatenate(
        [
            jnp.concatenate([pieces_ref[t, s, 0, p] for s in range(width)], 1)
            for p in range(part)
            for t in range(blocks)
        ],
        0,
    )
    chunk = math.gcd(length, 256)
    for at in range(0, length, chunk):
        cosine = jnp.dot(field, x_ref[:, at : at + chunk], preferred_element_type=jnp.float32)
        sine = jnp.dot(
            field, x_ref[:, length + at : length + at + chunk], preferred_element_type=jnp.float32
        )
        real_part = cosine[:all_frames] + sine[all_frames:]
        imag_part = cosine[all_frames:] - sine[:all_frames]
        modes = jnp.concatenate([real_part, imag_part], 0).astype(jnp.bfloat16)
        moved = jnp.dot(window_ref[...], modes, preferred_element_type=jnp.float32)
        power = moved * moved
        total = power[:size]
        for row in range(size, power.shape[0], size):
            total = total + power[row : row + size]
        total = total * scale
        own_ref[0, :, at : at + chunk] = total
        if mirrored:
            flipped = jnp.dot(
                flip_w_ref[...], total.astype(jnp.bfloat16), preferred_element_type=jnp.float32
            )
            row = pl.num_programs(0) - 1 - pl.program_id(0)
            scratch[row, :, at : at + chunk] = flipped.astype(jnp.bfloat16)
    if mirrored:

        @pl.when(pl.program_id(0) == pl.num_programs(0) - 1)
        def reverse():
            number = scratch.shape[0]
            flat = scratch[...].reshape(number * size, length)
            turned = jnp.dot(flat, flip_k_ref[...], preferred_element_type=jnp.float32)
            mirror_ref[...] = turned.astype(jnp.bfloat16).reshape(number, size, length)


def spectrum(pieces, tables, scale, mirrored):
    blocks, width, number, part, frames, rows = pieces.shape
    length = width * rows
    size = 2 * frames
    if rows != LANES:
        pieces = pieces.transpose(0, 2, 3, 4, 1, 5).reshape(blocks, 1, number, part, frames, length)
        width, rows = 1, length
    x_values, windows, flip_w, flip_k = tables
    whole = lambda array: pl.BlockSpec(array.shape, lambda i: (0,) * array.ndim)
    operands = [pieces, x_values, windows]
    in_specs = [
        pl.BlockSpec((blocks, width, 1, part, frames, rows), lambda i: (0, 0, i, 0, 0, 0)),
        whole(x_values),
        whole(windows),
    ]
    out_shape = [jax.ShapeDtypeStruct((number, size, length), jnp.float32)]
    out_specs = [pl.BlockSpec((1, size, length), lambda i: (i, 0, 0))]
    scratch_shapes = []
    if mirrored:
        operands += [flip_w, flip_k]
        in_specs += [whole(flip_w), whole(flip_k)]
        out_shape.append(jax.ShapeDtypeStruct((number, size, length), jnp.bfloat16))
        out_specs.append(pl.BlockSpec((number, size, length), lambda i: (0, 0, 0)))
        scratch_shapes.append(pltpu.VMEM((number, size, length), jnp.bfloat16))
    return pl.pallas_call(
        functools.partial(spectrum_kernel, scale, mirrored),
        out_shape=out_shape,
        grid=(number,),
        in_specs=in_specs,
        out_specs=out_specs,
        scratch_shapes=scratch_shapes,
        compiler_params=pltpu.CompilerParams(vmem_limit_bytes=VMEM_BYTES),
        cost_estimate=LARGE,
        name="spectrum",
    )(*operands)


def rows_kernel(places, aliased, *refs):
    planes, out_ref = refs[aliased:-1], refs[-1]
    for at in range(0, len(places), TILE):
        stack = [planes[which][plane].astype(jnp.float32) for which, plane in places[at : at + TILE]]
        out_ref[:, at : at + TILE] = jnp.swapaxes(jnp.stack(stack, 0), 0, 1)


def write_rows(given, arrays, places, start, total):
    _, size, length = arrays[0].shape
    step = 16
    used = sorted({which for which, _ in places})
    places = [(used.index(which), plane) for which, plane in places]
    block = start // len(places)
    return pl.pallas_call(
        functools.partial(rows_kernel, places, len(given)),
        out_shape=jax.ShapeDtypeStruct((size, total, length), jnp.float32),
        grid=(size // step,),
        in_specs=[pl.BlockSpec(memory_space=pl.ANY)] * len(given)
        + [
            pl.BlockSpec((arrays[which].shape[0], step, length), lambda i: (0, i, 0))
            for which in used
        ],
        out_specs=pl.BlockSpec((step, len(places), length), lambda i: (i, block, 0)),
        input_output_aliases={0: 0} if given else {},
        compiler_params=pltpu.CompilerParams(vmem_limit_bytes=VMEM_BYTES),
        name="write_rows",
    )(*given, *[arrays[which] for which in used])


def assemble(slots, planes, images):
    half = max(max(slot) for slot in slots)
    total = 2 * half
    arrays = planes + images
    places = [None] * total
    for which, slot in enumerate(slots):
        for plane, row in enumerate(slot):
            places[row] = (which, plane)
            if which < len(images):
                places[total - row] = (len(planes) + which, len(slot) - 1 - plane)
    late = min(row for row in range(total) if places[row][0] == len(arrays) - 1)
    late -= late % TILE
    while late % (total - late):
        late -= TILE
    given = []
    if late:
        given.append(write_rows([], arrays, places[:late], 0, total))
    return write_rows(given, arrays, places[late:], late, total)


def split_rows(half):
    rows = list(range(half - 1, 0, -1))
    parts = [len(rows) * share // 15 for share in SHARES]
    slots = [sorted(rows[lo:hi]) for lo, hi in zip([0] + parts, parts) if hi > lo]
    return slots + [[0, half]]


def body(heights):
    frames, rows_dev, length = heights.shape
    tm_count = lax.axis_size("tm")
    rows_count = lax.axis_size("rows")
    devices = tm_count * rows_count
    owned = length // devices
    windows, energy = window_table(frames, tm_count - 1)
    scale = 1.0 / ((tm_count - 1) * energy)
    tables = (x_table(length), windows, reversal(2 * frames), reversal(length))
    tables = tuple(jnp.asarray(table) for table in tables)
    opposite = [(device, devices - 1 - device) for device in range(devices)]

    def mix(heights, slot):
        wavenumbers = (np.arange(devices)[:, None] * owned + np.asarray(slot)[None, :]).reshape(-1)
        mixed = row_transform(heights, jnp.asarray(y_table(length, wavenumbers)))
        return mixed.reshape(devices, len(slot), 2, frames, rows_dev)

    def arrive(mixed):
        got = lax.all_to_all(mixed, AXES, split_axis=0, concat_axis=0, tiled=True)
        return got.reshape((tm_count, rows_count) + mixed.shape[1:])

    slots = split_rows(owned // 2)
    pieces = [arrive(mix(heights, slot)) for slot in slots[:2]]
    planes, images = [], []
    for at in range(len(slots) - 1):
        if images:
            pieces[at], images[-1] = lax.optimization_barrier((pieces[at], images[-1]))
        plane, image = spectrum(pieces[at], tables, scale, True)
        if at + 2 < len(slots):
            plane, image, later = lax.optimization_barrier((plane, image, heights))
            pieces.append(arrive(mix(later, slots[at + 2])))
        planes.append(plane)
        images.append(lax.ppermute(image, AXES, opposite))
    planes += spectrum(pieces[-1], tables, scale, False)
    return assemble(slots, planes, images)


def solution(mesh):
    in_specs = (P("tm", "rows", None),)
    out_specs = P(None, ("tm", "rows"), None)
    return jax.shard_map(body, mesh=mesh, in_specs=in_specs, out_specs=out_specs, check_vma=False)
```

```python
import functools
import math

import jax
import jax.numpy as jnp
import ml_dtypes
import numpy as np
from jax import lax
from jax.experimental import pallas as pl
from jax.experimental.pallas import tpu as pltpu
from jax.sharding import PartitionSpec as P

AXES = ("tm", "rows")
LANES = 128
TILE = 8
SHARES = (4, 11, 15)
SMALL = pl.CostEstimate(flops=1 << 20, bytes_accessed=1 << 20, transcendentals=0)
LARGE = pl.CostEstimate(flops=1 << 40, bytes_accessed=1 << 20, transcendentals=0)
VMEM_BYTES = 63 * 1024 * 1024
ROWS_VMEM_BYTES = 40 * 1024 * 1024
ROWS_STEP = 32


def to_bf16(values):
    return values.astype(ml_dtypes.bfloat16)


def unit_angles(left, right, modulus):
    return (np.outer(left, right) % modulus).astype(np.float32) * np.float32(2.0 * math.pi / modulus)


def y_table(length, wavenumbers, paired):
    angles = unit_angles(wavenumbers.reshape(-1), np.arange(length), length)
    pairs = np.stack([np.cos(angles), -np.sin(angles)], 1) / np.float32(math.sqrt(length))
    if paired is not None:
        pairs = pairs.reshape(wavenumbers.shape + (2, length))
        pairs[paired][1] = 1.0 / math.sqrt(length)
    return to_bf16(pairs.reshape(2 * wavenumbers.size, length))


def x_table(length):
    angles = unit_angles(np.arange(length), np.arange(length), length)
    return to_bf16(
        np.concatenate([np.cos(angles), np.sin(angles)], 1) / np.float32(math.sqrt(length))
    )


def window_table(hop, windows):
    size = 2 * hop
    steps = np.arange(size)
    hann = np.float32(0.5) - np.float32(0.5) * np.cos(
        steps.astype(np.float32) * np.float32(2.0 * math.pi / size)
    )
    angles = unit_angles(steps, steps, size)
    cosine = to_bf16(np.cos(angles) * hann[None, :])
    sine = to_bf16(np.sin(angles) * hann[None, :])
    frames = hop * (windows + 1)
    table = np.zeros((windows, 2, size, 2, frames), ml_dtypes.bfloat16)
    for window in range(windows):
        at = slice(window * hop, window * hop + size)
        table[window, 0, :, 0, at] = cosine
        table[window, 0, :, 1, at] = sine
        table[window, 1, :, 1, at] = cosine
        table[window, 1, :, 0, at] = -sine
    return table.reshape(windows * 2 * size, 2 * frames), float(np.sum(hann * hann))


def reversal(size):
    matrix = np.zeros((size, size), ml_dtypes.bfloat16)
    matrix[np.arange(size), (size - np.arange(size)) % size] = 1
    return matrix


def row_transform_kernel(table_ref, heights_ref, out_ref):
    frames, rows, length = heights_ref.shape
    planes = []
    for frame in range(0, frames, 2):
        pair = heights_ref[frame : frame + 2].reshape(2 * rows, length)
        product = lax.dot_general(
            table_ref[...], pair, (((1,), (1,)), ((), ())), preferred_element_type=jnp.float32
        )
        planes += [product[:, :rows], product[:, rows:]]
    out_ref[...] = jnp.swapaxes(jnp.stack(planes, 0), 0, 1).astype(jnp.bfloat16)


def row_transform(heights, table):
    frames, rows, length = heights.shape
    columns = table.shape[0]
    if rows != LANES:
        return jnp.einsum(
            "cy,fxy->cfx", table, heights, preferred_element_type=jnp.float32
        ).astype(jnp.bfloat16)
    step = 16
    return pl.pallas_call(
        row_transform_kernel,
        out_shape=jax.ShapeDtypeStruct((columns, frames, rows), jnp.bfloat16),
        grid=(frames // step,),
        in_specs=[
            pl.BlockSpec((columns, length), lambda i: (0, 0)),
            pl.BlockSpec((step, rows, length), lambda i: (i, 0, 0)),
        ],
        out_specs=pl.BlockSpec((columns, step, rows), lambda i: (0, i, 0)),
        compiler_params=pltpu.CompilerParams(vmem_limit_bytes=VMEM_BYTES),
        cost_estimate=SMALL,
        name="row_transform",
    )(table, heights)


def gather_field(pieces_ref):
    blocks, width, _, part, _, _ = pieces_ref.shape
    return jnp.concatenate(
        [
            jnp.concatenate([pieces_ref[t, s, 0, p] for s in range(width)], 1)
            for p in range(part)
            for t in range(blocks)
        ],
        0,
    )


def column_products(field, x_ref, at, chunk):
    length = x_ref.shape[0]
    return (
        jnp.dot(field, x_ref[:, at : at + chunk], preferred_element_type=jnp.float32),
        jnp.dot(
            field, x_ref[:, length + at : length + at + chunk], preferred_element_type=jnp.float32
        ),
    )


def mean_power(real_part, imag_part, window_ref, scale, size):
    modes = jnp.concatenate([real_part, imag_part], 0).astype(jnp.bfloat16)
    moved = jnp.dot(window_ref[...], modes, preferred_element_type=jnp.float32)
    power = moved * moved
    total = power[:size]
    for row in range(size, power.shape[0], size):
        total = total + power[row : row + size]
    return total * scale


def flipped(power, flip_w_ref):
    return jnp.dot(
        flip_w_ref[...], power.astype(jnp.bfloat16), preferred_element_type=jnp.float32
    ).astype(jnp.bfloat16)


def spectrum_kernel(
    scale, pieces_ref, x_ref, window_ref, flip_w_ref, flip_k_ref, own_ref, mirror_ref, scratch
):
    length = x_ref.shape[0]
    number, size, _ = scratch.shape
    field = gather_field(pieces_ref)
    frames = field.shape[0] // 2
    chunk = math.gcd(length, 256)
    for at in range(0, length, chunk):
        cosine, sine = column_products(field, x_ref, at, chunk)
        real_part = cosine[:frames] + sine[frames:]
        imag_part = cosine[frames:] - sine[:frames]
        total = mean_power(real_part, imag_part, window_ref, scale, size)
        own_ref[0, :, at : at + chunk] = total
        scratch[number - 1 - pl.program_id(0), :, at : at + chunk] = flipped(total, flip_w_ref)

    @pl.when(pl.program_id(0) == number - 1)
    def reverse():
        flat = scratch[...].reshape(number * size, length)
        turned = jnp.dot(flat, flip_k_ref[...], preferred_element_type=jnp.float32)
        mirror_ref[...] = turned.astype(jnp.bfloat16).reshape(number, size, length)


def edge_kernel(
    scale,
    paired_ref,
    pieces_ref,
    x_ref,
    window_ref,
    flip_w_ref,
    flip_k_ref,
    own_ref,
    mirror_ref,
    scratch,
):
    length = x_ref.shape[0]
    size = scratch.shape[1]
    paired = paired_ref[0] != 0
    apart = jnp.where(paired, 0.0, 1.0)
    field = gather_field(pieces_ref)
    frames = field.shape[0] // 2
    chunk = math.gcd(length, 256)
    for at in range(0, length, chunk):
        cosine, sine = column_products(field, x_ref, at, chunk)
        real_part = cosine[:frames] + apart * sine[frames:]
        imag_part = apart * cosine[frames:] - sine[:frames]
        total = mean_power(real_part, imag_part, window_ref, scale, size)
        other = mean_power(cosine[frames:], -sine[frames:], window_ref, scale, size)
        own_ref[0, :, at : at + chunk] = total
        mirror_ref[0, :, at : at + chunk] = other.astype(jnp.bfloat16)
        scratch[0, :, at : at + chunk] = flipped(total, flip_w_ref)

    @pl.when(jnp.logical_not(paired))
    def reverse():
        turned = jnp.dot(scratch[0], flip_k_ref[...], preferred_element_type=jnp.float32)
        mirror_ref[0] = turned.astype(jnp.bfloat16)


def spectrum(pieces, start, number, tables, scale, paired=None):
    blocks, width, _, part, frames, rows = pieces.shape
    length = width * rows
    size = 2 * frames
    if rows != LANES:
        pieces = pieces[:, :, start : start + number].transpose(0, 2, 3, 4, 1, 5)
        pieces = pieces.reshape(blocks, 1, number, part, frames, length)
        width, rows, start = 1, length, 0
    whole = lambda array: pl.BlockSpec(array.shape, lambda i, *_: (0,) * array.ndim)
    block = (blocks, width, 1, part, frames, rows)
    scalars = [] if paired is None else [paired]
    return pl.pallas_call(
        functools.partial(spectrum_kernel if paired is None else edge_kernel, scale),
        out_shape=[
            jax.ShapeDtypeStruct((number, size, length), jnp.float32),
            jax.ShapeDtypeStruct((number, size, length), jnp.bfloat16),
        ],
        grid_spec=pltpu.PrefetchScalarGridSpec(
            num_scalar_prefetch=len(scalars),
            grid=(number,),
            in_specs=[pl.BlockSpec(block, lambda i, *_: (0, 0, start + i, 0, 0, 0))]
            + [whole(table) for table in tables],
            out_specs=[
                pl.BlockSpec((1, size, length), lambda i, *_: (i, 0, 0)),
                pl.BlockSpec((number, size, length), lambda i, *_: (0, 0, 0)),
            ],
            scratch_shapes=[pltpu.VMEM((number, size, length), jnp.bfloat16)],
        ),
        compiler_params=pltpu.CompilerParams(vmem_limit_bytes=VMEM_BYTES),
        cost_estimate=LARGE if paired is None else SMALL,
        name="spectrum" if paired is None else "edge_spectrum",
    )(*scalars, pieces, *tables)


def rows_kernel(places, aliased, *refs):
    planes, out_ref = refs[aliased:-1], refs[-1]
    for at in range(0, len(places), TILE):
        stack = [planes[which][plane].astype(jnp.float32) for which, plane in places[at : at + TILE]]
        out_ref[:, at : at + TILE] = jnp.swapaxes(jnp.stack(stack, 0), 0, 1)


def write_rows(given, arrays, places, start, total):
    _, size, length = arrays[0].shape
    step = ROWS_STEP
    used = sorted({which for which, _ in places})
    places = [(used.index(which), plane) for which, plane in places]
    block = start // len(places)
    return pl.pallas_call(
        functools.partial(rows_kernel, places, len(given)),
        out_shape=jax.ShapeDtypeStruct((size, total, length), jnp.float32),
        grid=(size // step,),
        in_specs=[pl.BlockSpec(memory_space=pl.ANY)] * len(given)
        + [
            pl.BlockSpec((arrays[which].shape[0], step, length), lambda i: (0, i, 0))
            for which in used
        ],
        out_specs=pl.BlockSpec((step, len(places), length), lambda i: (i, block, 0)),
        input_output_aliases={0: 0} if given else {},
        compiler_params=pltpu.CompilerParams(vmem_limit_bytes=ROWS_VMEM_BYTES),
        name="write_rows",
    )(*given, *[arrays[which] for which in used])


def assemble(arrays, places, last):
    total = len(places)
    late = min(row for row in range(total) if places[row][0] == last)
    late -= late % TILE
    while late % (total - late):
        late -= TILE
    given = []
    if late:
        given.append(write_rows([], arrays, places[:late], 0, total))
    return write_rows(given, arrays, places[late:], late, total)


def split_rows(half):
    rows = list(range(half - 1, 0, -1))
    parts = [len(rows) * share // SHARES[-1] for share in SHARES]
    return [sorted(rows[lo:hi]) for lo, hi in zip([0] + parts, parts) if hi > lo]


def body(heights):
    frames, rows_dev, length = heights.shape
    tm_count = lax.axis_size("tm")
    rows_count = lax.axis_size("rows")
    devices = tm_count * rows_count
    owned = length // devices
    half = owned // 2
    middle = devices // 2
    windows, energy = window_table(frames, tm_count - 1)
    scale = 1.0 / ((tm_count - 1) * energy)
    tables = (x_table(length), windows, reversal(2 * frames), reversal(length))
    tables = tuple(jnp.asarray(table) for table in tables)
    device = lax.axis_index(AXES)
    opposite = [(d, devices - 1 - d) for d in range(devices)]
    edge_partner = [(d, devices - 1 - d if d < middle else (devices - d) % middle) for d in range(devices)]

    edges = np.array([d * owned + (half if d < middle else 0) for d in range(devices)])

    def mix(heights, slot, with_edge):
        wavenumbers = np.arange(devices)[:, None] * owned + np.asarray(slot)
        if with_edge:
            wavenumbers = np.concatenate([edges[:, None], wavenumbers], 1)
        table = y_table(length, wavenumbers, (middle, 0) if with_edge else None)
        mixed = row_transform(heights, jnp.asarray(table))
        return mixed.reshape(devices, -1, 2, frames, rows_dev)

    def arrive(mixed):
        got = lax.all_to_all(mixed, AXES, split_axis=0, concat_axis=0, tiled=True)
        return got.reshape((tm_count, rows_count) + mixed.shape[1:])

    slots = split_rows(half)
    pieces = [arrive(mix(heights, slot, at == 0)) for at, slot in enumerate(slots[:2])]
    paired = (device == middle).astype(jnp.int32).reshape(1)
    planes, images = [], []
    for at, slot in enumerate(slots):
        if 0 < at < len(slots) - 1:
            pieces[at], images, edge_image = lax.optimization_barrier(
                (pieces[at], images, edge_image)
            )
        plane, image = spectrum(pieces[at], int(at == 0), len(slot), tables, scale)
        if at == 0:
            edge, edge_image = spectrum(pieces[0], 0, 1, tables, scale, paired)
            edge_image = lax.ppermute(edge_image, AXES, edge_partner)
        if at + 2 < len(slots):
            plane, image, later = lax.optimization_barrier((plane, image, heights))
            pieces.append(arrive(mix(later, slots[at + 2], False)))
        planes.append(plane)
        images.append(lax.ppermute(image, AXES, opposite))
    edge_image = edge_image.astype(jnp.float32)
    lower = device < middle
    arrays = planes + images
    last = len(arrays) - 1
    arrays += [jnp.where(lower, edge_image, edge), jnp.where(lower, edge, edge_image)]
    places = [None] * owned
    places[0], places[half] = (last + 1, 0), (last + 2, 0)
    for at, slot in enumerate(slots):
        for plane, row in enumerate(slot):
            places[row] = (at, plane)
            places[owned - row] = (len(slots) + at, len(slot) - 1 - plane)
    return assemble(arrays, places, last)


def solution(mesh):
    in_specs = (P("tm", "rows", None),)
    out_specs = P(None, ("tm", "rows"), None)
    return jax.shard_map(body, mesh=mesh, in_specs=in_specs, out_specs=out_specs, check_vma=False)
```

```python
import functools
import math

import jax
import jax.numpy as jnp
import ml_dtypes
import numpy as np
from jax import lax
from jax.experimental import pallas as pl
from jax.experimental.pallas import tpu as pltpu
from jax.sharding import PartitionSpec as P

AXES = ("tm", "half", "near")
LANES = 128
TILE = 8
SHARES = (9, 11, 15)
SMALL = pl.CostEstimate(flops=1 << 20, bytes_accessed=1 << 20, transcendentals=0)
LARGE = pl.CostEstimate(flops=1 << 40, bytes_accessed=1 << 20, transcendentals=0)
VMEM_BYTES = 63 * 1024 * 1024
ROWS_VMEM_BYTES = 40 * 1024 * 1024
ROWS_STEP = 32


def to_bf16(values):
    return values.astype(ml_dtypes.bfloat16)


def unit_angles(left, right, modulus):
    return (np.outer(left, right) % modulus).astype(np.float32) * np.float32(2.0 * math.pi / modulus)


def y_table(length, wavenumbers, paired):
    angles = unit_angles(wavenumbers.reshape(-1), np.arange(length), length)
    pairs = np.stack([np.cos(angles), -np.sin(angles)], 1) / np.float32(math.sqrt(length))
    if paired is not None:
        pairs = pairs.reshape(wavenumbers.shape + (2, length))
        pairs[paired][1] = 1.0 / math.sqrt(length)
    return to_bf16(pairs.reshape(2 * wavenumbers.size, length))


def x_table(length):
    angles = unit_angles(np.arange(length), np.arange(length), length)
    return to_bf16(
        np.concatenate([np.cos(angles), np.sin(angles)], 1) / np.float32(math.sqrt(length))
    )


def window_table(hop, windows):
    size = 2 * hop
    steps = np.arange(size)
    hann = np.float32(0.5) - np.float32(0.5) * np.cos(
        steps.astype(np.float32) * np.float32(2.0 * math.pi / size)
    )
    angles = unit_angles(steps, steps, size)
    cosine = to_bf16(np.cos(angles) * hann[None, :])
    sine = to_bf16(np.sin(angles) * hann[None, :])
    frames = hop * (windows + 1)
    table = np.zeros((windows, 2, size, 2, frames), ml_dtypes.bfloat16)
    for window in range(windows):
        at = slice(window * hop, window * hop + size)
        table[window, 0, :, 0, at] = cosine
        table[window, 0, :, 1, at] = sine
        table[window, 1, :, 1, at] = cosine
        table[window, 1, :, 0, at] = -sine
    return table.reshape(windows * 2 * size, 2 * frames), float(np.sum(hann * hann))


def reversal(size):
    matrix = np.zeros((size, size), ml_dtypes.bfloat16)
    matrix[np.arange(size), (size - np.arange(size)) % size] = 1
    return matrix


def row_transform_kernel(which_ref, table_ref, heights_ref, out_ref):
    del which_ref
    frames, rows, length = heights_ref.shape
    planes = []
    for frame in range(0, frames, 2):
        pair = heights_ref[frame : frame + 2].reshape(2 * rows, length)
        product = lax.dot_general(
            table_ref[0], pair, (((1,), (1,)), ((), ())), preferred_element_type=jnp.float32
        )
        planes += [product[:, :rows], product[:, rows:]]
    out_ref[...] = jnp.swapaxes(jnp.stack(planes, 0), 0, 1).astype(jnp.bfloat16)


def row_transform(which, heights, table, cost):
    frames, rows, length = heights.shape
    columns = table.shape[1]
    if rows != LANES:
        picked = lax.dynamic_index_in_dim(table, which, 0, keepdims=False)
        return jnp.einsum(
            "cy,fxy->cfx", picked, heights, preferred_element_type=jnp.float32
        ).astype(jnp.bfloat16)
    step = 16
    return pl.pallas_call(
        row_transform_kernel,
        out_shape=jax.ShapeDtypeStruct((columns, frames, rows), jnp.bfloat16),
        grid_spec=pltpu.PrefetchScalarGridSpec(
            num_scalar_prefetch=1,
            grid=(frames // step,),
            in_specs=[
                pl.BlockSpec((1, columns, length), lambda i, which_ref: (which_ref[0], 0, 0)),
                pl.BlockSpec((step, rows, length), lambda i, which_ref: (i, 0, 0)),
            ],
            out_specs=pl.BlockSpec((columns, step, rows), lambda i, which_ref: (0, i, 0)),
        ),
        compiler_params=pltpu.CompilerParams(vmem_limit_bytes=VMEM_BYTES),
        cost_estimate=cost,
        name="row_transform",
    )(jnp.asarray(which, jnp.int32).reshape(1), table, heights)


def gather_field(pieces_ref):
    blocks, width, _, part, _, _ = pieces_ref.shape
    return jnp.concatenate(
        [
            jnp.concatenate([pieces_ref[t, s, 0, p] for s in range(width)], 1)
            for p in range(part)
            for t in range(blocks)
        ],
        0,
    )


def column_products(field, x_ref, at, chunk):
    length = x_ref.shape[0]
    return (
        jnp.dot(field, x_ref[:, at : at + chunk], preferred_element_type=jnp.float32),
        jnp.dot(
            field, x_ref[:, length + at : length + at + chunk], preferred_element_type=jnp.float32
        ),
    )


def mean_power(real_part, imag_part, window_ref, scale, size):
    modes = jnp.concatenate([real_part, imag_part], 0).astype(jnp.bfloat16)
    moved = jnp.dot(window_ref[...], modes, preferred_element_type=jnp.float32)
    power = moved * moved
    total = power[:size]
    for row in range(size, power.shape[0], size):
        total = total + power[row : row + size]
    return total * scale


def flipped(power, flip_w_ref):
    return jnp.dot(
        flip_w_ref[...], power.astype(jnp.bfloat16), preferred_element_type=jnp.float32
    ).astype(jnp.bfloat16)


def spectrum_kernel(
    scale, pieces_ref, x_ref, window_ref, flip_w_ref, flip_k_ref, own_ref, mirror_ref, scratch
):
    length = x_ref.shape[0]
    number, size, _ = scratch.shape
    field = gather_field(pieces_ref)
    frames = field.shape[0] // 2
    chunk = length
    for at in range(0, length, chunk):
        cosine, sine = column_products(field, x_ref, at, chunk)
        real_part = cosine[:frames] + sine[frames:]
        imag_part = cosine[frames:] - sine[:frames]
        total = mean_power(real_part, imag_part, window_ref, scale, size)
        own_ref[0, :, at : at + chunk] = total
        scratch[number - 1 - pl.program_id(0), :, at : at + chunk] = flipped(total, flip_w_ref)

    @pl.when(pl.program_id(0) == number - 1)
    def reverse():
        flat = scratch[...].reshape(number * size, length)
        turned = jnp.dot(flat, flip_k_ref[...], preferred_element_type=jnp.float32)
        mirror_ref[...] = turned.astype(jnp.bfloat16).reshape(number, size, length)


def edge_kernel(
    scale,
    paired_ref,
    pieces_ref,
    x_ref,
    window_ref,
    flip_w_ref,
    flip_k_ref,
    own_ref,
    mirror_ref,
    scratch,
):
    length = x_ref.shape[0]
    size = scratch.shape[1]
    paired = paired_ref[0] != 0
    apart = jnp.where(paired, 0.0, 1.0)
    field = gather_field(pieces_ref)
    frames = field.shape[0] // 2
    chunk = length
    for at in range(0, length, chunk):
        cosine, sine = column_products(field, x_ref, at, chunk)
        real_part = cosine[:frames] + apart * sine[frames:]
        imag_part = apart * cosine[frames:] - sine[:frames]
        total = mean_power(real_part, imag_part, window_ref, scale, size)
        other = mean_power(cosine[frames:], -sine[frames:], window_ref, scale, size)
        own_ref[0, :, at : at + chunk] = total
        mirror_ref[0, :, at : at + chunk] = other.astype(jnp.bfloat16)
        scratch[0, :, at : at + chunk] = flipped(total, flip_w_ref)

    @pl.when(jnp.logical_not(paired))
    def reverse():
        turned = jnp.dot(scratch[0], flip_k_ref[...], preferred_element_type=jnp.float32)
        mirror_ref[0] = turned.astype(jnp.bfloat16)


def spectrum(pieces, start, number, tables, scale, cost, paired=None):
    blocks, width, _, part, frames, rows = pieces.shape
    length = width * rows
    size = 2 * frames
    if rows != LANES:
        pieces = pieces[:, :, start : start + number].transpose(0, 2, 3, 4, 1, 5)
        pieces = pieces.reshape(blocks, 1, number, part, frames, length)
        width, rows, start = 1, length, 0
    whole = lambda array: pl.BlockSpec(array.shape, lambda i, *_: (0,) * array.ndim)
    block = (blocks, width, 1, part, frames, rows)
    scalars = [] if paired is None else [paired]
    return pl.pallas_call(
        functools.partial(spectrum_kernel if paired is None else edge_kernel, scale),
        out_shape=[
            jax.ShapeDtypeStruct((number, size, length), jnp.float32),
            jax.ShapeDtypeStruct((number, size, length), jnp.bfloat16),
        ],
        grid_spec=pltpu.PrefetchScalarGridSpec(
            num_scalar_prefetch=len(scalars),
            grid=(number,),
            in_specs=[pl.BlockSpec(block, lambda i, *_: (0, 0, start + i, 0, 0, 0))]
            + [whole(table) for table in tables],
            out_specs=[
                pl.BlockSpec((1, size, length), lambda i, *_: (i, 0, 0)),
                pl.BlockSpec((number, size, length), lambda i, *_: (0, 0, 0)),
            ],
            scratch_shapes=[pltpu.VMEM((number, size, length), jnp.bfloat16)],
        ),
        compiler_params=pltpu.CompilerParams(vmem_limit_bytes=VMEM_BYTES),
        cost_estimate=cost,
        name="spectrum" if paired is None else "edge_spectrum",
    )(*scalars, pieces, *tables)


def rows_kernel(places, aliased, *refs):
    planes, out_ref = refs[aliased:-1], refs[-1]
    for at in range(0, len(places), TILE):
        stack = [planes[which][plane].astype(jnp.float32) for which, plane in places[at : at + TILE]]
        out_ref[:, at : at + TILE] = jnp.swapaxes(jnp.stack(stack, 0), 0, 1)


def write_rows(given, arrays, places, start, total):
    _, size, length = arrays[0].shape
    step = ROWS_STEP
    used = sorted({which for which, _ in places})
    places = [(used.index(which), plane) for which, plane in places]
    block = start // len(places)
    return pl.pallas_call(
        functools.partial(rows_kernel, places, len(given)),
        out_shape=jax.ShapeDtypeStruct((size, total, length), jnp.float32),
        grid=(size // step,),
        in_specs=[pl.BlockSpec(memory_space=pl.ANY)] * len(given)
        + [
            pl.BlockSpec((arrays[which].shape[0], step, length), lambda i: (0, i, 0))
            for which in used
        ],
        out_specs=pl.BlockSpec((step, len(places), length), lambda i: (i, block, 0)),
        input_output_aliases={0: 0} if given else {},
        compiler_params=pltpu.CompilerParams(vmem_limit_bytes=ROWS_VMEM_BYTES),
        name="write_rows",
    )(*given, *[arrays[which] for which in used])


def assemble(arrays, places):
    total = len(places)
    late = total // 2 if total // 2 % TILE == 0 else 0
    given = []
    if late:
        given.append(write_rows([], arrays, places[:late], 0, total))
    return write_rows(given, arrays, places[late:], late, total)


def split_rows(half):
    rows = list(range(half - 1, 0, -1))
    parts = [0] + [len(rows) * share // SHARES[-1] for share in SHARES]
    return [sorted(rows[lo:hi]) for lo, hi in zip(parts, parts[1:])]


def exchange(blocks, axis, dim):
    count = lax.axis_size(axis)
    me = lax.axis_index(axis)
    pick = lambda at: lax.dynamic_index_in_dim(blocks, at, dim)
    moved = [pick(me)]
    for shift in range(1, count):
        to = [(i, (i + shift) % count) for i in range(count)]
        moved.append(lax.ppermute(pick((me + shift) % count), axis, to))
    rising = moved[:1] + moved[:0:-1]
    joined = jnp.concatenate(rising + rising[:-1], dim)
    return lax.dynamic_slice_in_dim(joined, (count - me) % count, count, dim)


def body(heights):
    frames, rows_dev, length = heights.shape
    tm_count = lax.axis_size("tm")
    near_count = lax.axis_size("near")
    rows_count = 2 * near_count
    devices = tm_count * rows_count
    owned = length // devices
    half = owned // 2
    middle = devices // 2
    windows, energy = window_table(frames, tm_count - 1)
    scale = 1.0 / ((tm_count - 1) * energy)
    tables = (x_table(length), windows, reversal(2 * frames), reversal(length))
    tables = tuple(jnp.asarray(table) for table in tables)
    device = lax.axis_index(AXES)
    opposite = [(d, devices - 1 - d) for d in range(devices)]
    edge_partner = [(d, devices - 1 - d if d < middle else (devices - d) % middle) for d in range(devices)]

    edges = np.array([d * owned + (half if d < middle else 0) for d in range(devices)])

    def mix(heights, slot, with_edge, cost):
        wavenumbers = np.arange(devices)[:, None] * owned + np.asarray(slot)
        if with_edge:
            wavenumbers = np.concatenate([edges[:, None], wavenumbers], 1)
        table = y_table(length, wavenumbers, (middle, 0) if with_edge else None)
        mixed = row_transform(0, heights, jnp.asarray(table)[None], cost)
        return mixed.reshape(devices, -1, 2, frames, rows_dev)

    def arrive(mixed):
        got = lax.all_to_all(mixed, AXES, split_axis=0, concat_axis=0, tiled=True)
        return got.reshape((tm_count, rows_count) + mixed.shape[1:])

    def image_of(image, partner):
        return lax.ppermute(image, AXES, partner)

    slots = split_rows(half)
    paired = (device == middle).astype(jnp.int32).reshape(1)
    planes, images = {}, {}

    def powers(pieces, start, at, cost):
        if slots[at]:
            planes[at], image = spectrum(pieces, start, len(slots[at]), tables, scale, cost)
            images[at] = image_of(image, opposite)

    def mix_half(heights, slot, which):
        receivers = np.arange(devices).reshape(tm_count, 2, near_count).transpose(1, 0, 2)
        wavenumbers = receivers[..., None] * owned + np.asarray(slot)
        table = y_table(length, wavenumbers, None).reshape(2, -1, length)
        mixed = row_transform(which, heights, jnp.asarray(table), SMALL)
        return mixed.reshape(tm_count, 1, near_count, len(slot), 2, frames, rows_dev)

    later = heights
    side = lax.axis_index("half")
    if slots[1]:
        away, later = lax.optimization_barrier((mix_half(later, slots[1], 1 - side), later))
        away = lax.ppermute(away, "half", [(0, 1), (1, 0)])
    first, later = lax.optimization_barrier((mix(later, slots[0], True, SMALL), later))
    second, later = lax.optimization_barrier((mix(later, slots[2], False, LARGE), later))
    if slots[1]:
        away, later = lax.optimization_barrier((away, later))
        home = mix_half(later, slots[1], side)
        aside = jnp.concatenate([home, away, home], 1)
        aside = lax.dynamic_slice_in_dim(aside, side, 2, 1)
        aside = exchange(exchange(aside, "near", 2), "tm", 0)
        aside = aside.reshape((tm_count, rows_count) + aside.shape[3:])
    first = arrive(first)
    second = arrive(second)
    edge, edge_image = spectrum(first, 0, 1, tables, scale, SMALL, paired)
    edge_image = image_of(edge_image, edge_partner)
    first, edge = lax.optimization_barrier((first, edge))
    if slots[1]:
        first, aside = lax.optimization_barrier((first, aside))
    powers(first, 1, 0, LARGE)
    if slots[1]:
        powers(aside, 0, 1, SMALL)
    second, edge_image, planes = lax.optimization_barrier((second, edge_image, planes))
    powers(second, 0, 2, LARGE)
    edge_image = edge_image.astype(jnp.float32)
    lower = device < middle
    arrays = [planes[at] for at in sorted(planes)] + [images[at] for at in sorted(images)]
    last = len(arrays) - 1
    arrays += [jnp.where(lower, edge_image, edge), jnp.where(lower, edge, edge_image)]
    places = [None] * owned
    places[0], places[half] = (last + 1, 0), (last + 2, 0)
    for at, slot in enumerate([slot for slot in slots if slot]):
        for plane, row in enumerate(slot):
            places[row] = (at, plane)
            places[owned - row] = (len(planes) + at, len(slot) - 1 - plane)
    return assemble(arrays, places)


def solution(mesh):
    tm_count, rows_count = mesh.devices.shape
    split = jax.sharding.Mesh(
        mesh.devices.reshape(tm_count, 2, rows_count // 2), ("tm", "half", "near")
    )
    in_specs = (P("tm", ("half", "near"), None),)
    out_specs = P(None, AXES, None)
    return jax.shard_map(body, mesh=split, in_specs=in_specs, out_specs=out_specs, check_vma=False)
```

```python
import functools
import math

import jax
import jax.numpy as jnp
import ml_dtypes
import numpy as np
from jax import lax
from jax.experimental import pallas as pl
from jax.experimental.pallas import tpu as pltpu
from jax.sharding import PartitionSpec as P

AXES = ("tm", "half", "near")
LANES = 128
TILE = 8
SHARES = (8, 10, 11, 15)
SMALL = pl.CostEstimate(flops=1 << 20, bytes_accessed=1 << 20, transcendentals=0)
LARGE = pl.CostEstimate(flops=1 << 40, bytes_accessed=1 << 20, transcendentals=0)
VMEM_BYTES = 63 * 1024 * 1024
ROWS_VMEM_BYTES = 40 * 1024 * 1024
ROWS_STEP = 32


def to_bf16(values):
    return values.astype(ml_dtypes.bfloat16)


def unit_angles(left, right, modulus):
    return (np.outer(left, right) % modulus).astype(np.float32) * np.float32(2.0 * math.pi / modulus)


def y_table(length, wavenumbers, paired):
    angles = unit_angles(wavenumbers.reshape(-1), np.arange(length), length)
    pairs = np.stack([np.cos(angles), -np.sin(angles)], 1) / np.float32(math.sqrt(length))
    if paired is not None:
        pairs = pairs.reshape(wavenumbers.shape + (2, length))
        pairs[paired][1] = 1.0 / math.sqrt(length)
    return to_bf16(pairs.reshape(2 * wavenumbers.size, length))


def x_table(length):
    angles = unit_angles(np.arange(length), np.arange(length), length)
    return to_bf16(
        np.concatenate([np.cos(angles), np.sin(angles)], 1) / np.float32(math.sqrt(length))
    )


def window_table(hop, windows):
    size = 2 * hop
    steps = np.arange(size)
    hann = np.float32(0.5) - np.float32(0.5) * np.cos(
        steps.astype(np.float32) * np.float32(2.0 * math.pi / size)
    )
    angles = unit_angles(steps, steps, size)
    cosine = to_bf16(np.cos(angles) * hann[None, :])
    sine = to_bf16(np.sin(angles) * hann[None, :])
    frames = hop * (windows + 1)
    table = np.zeros((windows, 2, size, 2, frames), ml_dtypes.bfloat16)
    for window in range(windows):
        at = slice(window * hop, window * hop + size)
        table[window, 0, :, 0, at] = cosine
        table[window, 0, :, 1, at] = sine
        table[window, 1, :, 1, at] = cosine
        table[window, 1, :, 0, at] = -sine
    return table.reshape(windows * 2 * size, 2 * frames), float(np.sum(hann * hann))


def reversal(size):
    matrix = np.zeros((size, size), ml_dtypes.bfloat16)
    matrix[np.arange(size), (size - np.arange(size)) % size] = 1
    return matrix


def row_transform_kernel(which_ref, table_ref, heights_ref, out_ref):
    del which_ref
    frames, rows, length = heights_ref.shape
    planes = []
    for frame in range(0, frames, 2):
        pair = heights_ref[frame : frame + 2].reshape(2 * rows, length)
        product = lax.dot_general(
            table_ref[0], pair, (((1,), (1,)), ((), ())), preferred_element_type=jnp.float32
        )
        planes += [product[:, :rows], product[:, rows:]]
    out_ref[...] = jnp.swapaxes(jnp.stack(planes, 0), 0, 1).astype(jnp.bfloat16)


def row_transform(which, heights, table, cost):
    frames, rows, length = heights.shape
    columns = table.shape[1]
    if rows != LANES:
        picked = lax.dynamic_index_in_dim(table, which, 0, keepdims=False)
        return jnp.einsum(
            "cy,fxy->cfx", picked, heights, preferred_element_type=jnp.float32
        ).astype(jnp.bfloat16)
    step = 16
    return pl.pallas_call(
        row_transform_kernel,
        out_shape=jax.ShapeDtypeStruct((columns, frames, rows), jnp.bfloat16),
        grid_spec=pltpu.PrefetchScalarGridSpec(
            num_scalar_prefetch=1,
            grid=(frames // step,),
            in_specs=[
                pl.BlockSpec((1, columns, length), lambda i, which_ref: (which_ref[0], 0, 0)),
                pl.BlockSpec((step, rows, length), lambda i, which_ref: (i, 0, 0)),
            ],
            out_specs=pl.BlockSpec((columns, step, rows), lambda i, which_ref: (0, i, 0)),
        ),
        compiler_params=pltpu.CompilerParams(vmem_limit_bytes=VMEM_BYTES),
        cost_estimate=cost,
        name="row_transform",
    )(jnp.asarray(which, jnp.int32).reshape(1), table, heights)


def gather_field(pieces_ref):
    blocks, width, _, part, _, _ = pieces_ref.shape
    return jnp.concatenate(
        [
            jnp.concatenate([pieces_ref[t, s, 0, p] for s in range(width)], 1)
            for p in range(part)
            for t in range(blocks)
        ],
        0,
    )


def column_products(field, x_ref, at, chunk):
    length = x_ref.shape[0]
    return (
        jnp.dot(field, x_ref[:, at : at + chunk], preferred_element_type=jnp.float32),
        jnp.dot(
            field, x_ref[:, length + at : length + at + chunk], preferred_element_type=jnp.float32
        ),
    )


def mean_power(real_part, imag_part, window_ref, scale, size):
    modes = jnp.concatenate([real_part, imag_part], 0).astype(jnp.bfloat16)
    moved = jnp.dot(window_ref[...], modes, preferred_element_type=jnp.float32)
    power = moved * moved
    total = power[:size]
    for row in range(size, power.shape[0], size):
        total = total + power[row : row + size]
    return total * scale


def flipped(power, flip_w_ref):
    return jnp.dot(
        flip_w_ref[...], power.astype(jnp.bfloat16), preferred_element_type=jnp.float32
    ).astype(jnp.bfloat16)


def spectrum_kernel(
    scale, pieces_ref, x_ref, window_ref, flip_w_ref, flip_k_ref, own_ref, mirror_ref, scratch
):
    length = x_ref.shape[0]
    number, size, _ = scratch.shape
    field = gather_field(pieces_ref)
    frames = field.shape[0] // 2
    chunk = length
    for at in range(0, length, chunk):
        cosine, sine = column_products(field, x_ref, at, chunk)
        real_part = cosine[:frames] + sine[frames:]
        imag_part = cosine[frames:] - sine[:frames]
        total = mean_power(real_part, imag_part, window_ref, scale, size)
        own_ref[0, :, at : at + chunk] = total
        scratch[number - 1 - pl.program_id(0), :, at : at + chunk] = flipped(total, flip_w_ref)

    @pl.when(pl.program_id(0) == number - 1)
    def reverse():
        flat = scratch[...].reshape(number * size, length)
        turned = jnp.dot(flat, flip_k_ref[...], preferred_element_type=jnp.float32)
        mirror_ref[...] = turned.astype(jnp.bfloat16).reshape(number, size, length)


def edge_kernel(
    scale,
    paired_ref,
    pieces_ref,
    x_ref,
    window_ref,
    flip_w_ref,
    flip_k_ref,
    own_ref,
    mirror_ref,
    scratch,
):
    length = x_ref.shape[0]
    size = scratch.shape[1]
    paired = paired_ref[0] != 0
    apart = jnp.where(paired, 0.0, 1.0)
    field = gather_field(pieces_ref)
    frames = field.shape[0] // 2
    chunk = length
    for at in range(0, length, chunk):
        cosine, sine = column_products(field, x_ref, at, chunk)
        real_part = cosine[:frames] + apart * sine[frames:]
        imag_part = apart * cosine[frames:] - sine[:frames]
        total = mean_power(real_part, imag_part, window_ref, scale, size)
        other = mean_power(cosine[frames:], -sine[frames:], window_ref, scale, size)
        own_ref[0, :, at : at + chunk] = total
        mirror_ref[0, :, at : at + chunk] = other.astype(jnp.bfloat16)
        scratch[0, :, at : at + chunk] = flipped(total, flip_w_ref)

    @pl.when(jnp.logical_not(paired))
    def reverse():
        turned = jnp.dot(scratch[0], flip_k_ref[...], preferred_element_type=jnp.float32)
        mirror_ref[0] = turned.astype(jnp.bfloat16)


def spectrum(pieces, start, number, tables, scale, cost, paired=None):
    blocks, width, _, part, frames, rows = pieces.shape
    length = width * rows
    size = 2 * frames
    if rows != LANES:
        pieces = pieces[:, :, start : start + number].transpose(0, 2, 3, 4, 1, 5)
        pieces = pieces.reshape(blocks, 1, number, part, frames, length)
        width, rows, start = 1, length, 0
    whole = lambda array: pl.BlockSpec(array.shape, lambda i, *_: (0,) * array.ndim)
    block = (blocks, width, 1, part, frames, rows)
    scalars = [] if paired is None else [paired]
    return pl.pallas_call(
        functools.partial(spectrum_kernel if paired is None else edge_kernel, scale),
        out_shape=[
            jax.ShapeDtypeStruct((number, size, length), jnp.float32),
            jax.ShapeDtypeStruct((number, size, length), jnp.bfloat16),
        ],
        grid_spec=pltpu.PrefetchScalarGridSpec(
            num_scalar_prefetch=len(scalars),
            grid=(number,),
            in_specs=[pl.BlockSpec(block, lambda i, *_: (0, 0, start + i, 0, 0, 0))]
            + [whole(table) for table in tables],
            out_specs=[
                pl.BlockSpec((1, size, length), lambda i, *_: (i, 0, 0)),
                pl.BlockSpec((number, size, length), lambda i, *_: (0, 0, 0)),
            ],
            scratch_shapes=[pltpu.VMEM((number, size, length), jnp.bfloat16)],
        ),
        compiler_params=pltpu.CompilerParams(vmem_limit_bytes=VMEM_BYTES),
        cost_estimate=cost,
        name="spectrum" if paired is None else "edge_spectrum",
    )(*scalars, pieces, *tables)


def rows_kernel(places, aliased, *refs):
    planes, out_ref = refs[aliased:-1], refs[-1]
    for at in range(0, len(places), TILE):
        stack = [planes[which][plane].astype(jnp.float32) for which, plane in places[at : at + TILE]]
        out_ref[:, at : at + TILE] = jnp.swapaxes(jnp.stack(stack, 0), 0, 1)


def write_rows(given, arrays, places, start, total):
    _, size, length = arrays[0].shape
    step = ROWS_STEP
    used = sorted({which for which, _ in places})
    places = [(used.index(which), plane) for which, plane in places]
    block = start // len(places)
    return pl.pallas_call(
        functools.partial(rows_kernel, places, len(given)),
        out_shape=jax.ShapeDtypeStruct((size, total, length), jnp.float32),
        grid=(size // step,),
        in_specs=[pl.BlockSpec(memory_space=pl.ANY)] * len(given)
        + [
            pl.BlockSpec((arrays[which].shape[0], step, length), lambda i: (0, i, 0))
            for which in used
        ],
        out_specs=pl.BlockSpec((step, len(places), length), lambda i: (i, block, 0)),
        input_output_aliases={0: 0} if given else {},
        compiler_params=pltpu.CompilerParams(vmem_limit_bytes=ROWS_VMEM_BYTES),
        name="write_rows",
    )(*given, *[arrays[which] for which in used])


def assemble(arrays, places):
    total = len(places)
    late = total // 2 if total // 2 % TILE == 0 else 0
    given = []
    if late:
        given.append(write_rows([], arrays, places[:late], 0, total))
    return write_rows(given, arrays, places[late:], late, total)


def split_rows(half):
    rows = list(range(half - 1, 0, -1))
    parts = [0] + [len(rows) * share // SHARES[-1] for share in SHARES]
    return [sorted(rows[lo:hi]) for lo, hi in zip(parts, parts[1:])]


def exchange(blocks, axis, dim):
    count = lax.axis_size(axis)
    me = lax.axis_index(axis)
    pick = lambda at: lax.dynamic_index_in_dim(blocks, at, dim)
    moved = [pick(me)]
    for shift in range(1, count):
        to = [(i, (i + shift) % count) for i in range(count)]
        moved.append(lax.ppermute(pick((me + shift) % count), axis, to))
    rising = moved[:1] + moved[:0:-1]
    joined = jnp.concatenate(rising + rising[:-1], dim)
    return lax.dynamic_slice_in_dim(joined, (count - me) % count, count, dim)


def body(heights):
    frames, rows_dev, length = heights.shape
    tm_count = lax.axis_size("tm")
    near_count = lax.axis_size("near")
    rows_count = 2 * near_count
    devices = tm_count * rows_count
    owned = length // devices
    half = owned // 2
    middle = devices // 2
    windows, energy = window_table(frames, tm_count - 1)
    scale = 1.0 / ((tm_count - 1) * energy)
    tables = (x_table(length), windows, reversal(2 * frames), reversal(length))
    tables = tuple(jnp.asarray(table) for table in tables)
    device = lax.axis_index(AXES)
    opposite = [(d, devices - 1 - d) for d in range(devices)]
    edge_partner = [(d, devices - 1 - d if d < middle else (devices - d) % middle) for d in range(devices)]

    edges = np.array([d * owned + (half if d < middle else 0) for d in range(devices)])

    def mix(heights, slot, with_edge, cost):
        wavenumbers = np.arange(devices)[:, None] * owned + np.asarray(slot)
        if with_edge:
            wavenumbers = np.concatenate([edges[:, None], wavenumbers], 1)
        table = y_table(length, wavenumbers, (middle, 0) if with_edge else None)
        mixed = row_transform(0, heights, jnp.asarray(table)[None], cost)
        return mixed.reshape(devices, -1, 2, frames, rows_dev)

    def arrive(mixed):
        got = lax.all_to_all(mixed, AXES, split_axis=0, concat_axis=0, tiled=True)
        return got.reshape((tm_count, rows_count) + mixed.shape[1:])

    def image_of(image, partner):
        return lax.ppermute(image, AXES, partner)

    slots = split_rows(half)
    paired = (device == middle).astype(jnp.int32).reshape(1)
    planes, images = {}, {}

    def powers(pieces, start, at, cost):
        if slots[at]:
            planes[at], image = spectrum(pieces, start, len(slots[at]), tables, scale, cost)
            images[at] = image_of(image, opposite)

    def mix_half(heights, slot, which):
        receivers = np.arange(devices).reshape(tm_count, 2, near_count).transpose(1, 0, 2)
        wavenumbers = receivers[..., None] * owned + np.asarray(slot)
        table = y_table(length, wavenumbers, None).reshape(2, -1, length)
        mixed = row_transform(which, heights, jnp.asarray(table), SMALL)
        return mixed.reshape(tm_count, 1, near_count, len(slot), 2, frames, rows_dev)

    def joined(home, away):
        return lax.dynamic_slice_in_dim(jnp.concatenate([home, away, home], 1), side, 2, 1)

    def swapped(away):
        return lax.ppermute(away, "half", [(0, 1), (1, 0)])

    def pieces_of(parts):
        parts = exchange(parts, "tm", 0)
        return parts.reshape((tm_count, rows_count) + parts.shape[3:])

    later = heights
    side = lax.axis_index("half")
    if slots[1]:
        aside, later = lax.optimization_barrier((mix_half(later, slots[1], 1 - side), later))
        aside = swapped(aside)
    first, later = lax.optimization_barrier((mix(later, slots[0], True, SMALL), later))
    second, later = lax.optimization_barrier((mix(later, slots[3], False, LARGE), later))
    if slots[1]:
        aside, later = lax.optimization_barrier((aside, later))
        aside = exchange(joined(mix_half(later, slots[1], side), aside), "near", 2)
    if slots[2]:
        late, late_home = mix_half(later, slots[2], 1 - side), mix_half(later, slots[2], side)
        if slots[1]:
            late, late_home, aside = lax.optimization_barrier((late, late_home, aside))
        late = swapped(late)
    if slots[1]:
        aside = pieces_of(aside)
    first = arrive(first)
    second = arrive(second)
    edge, edge_image = spectrum(first, 0, 1, tables, scale, SMALL, paired)
    edge_image = image_of(edge_image, edge_partner)
    first, edge = lax.optimization_barrier((first, edge))
    if slots[1]:
        first, aside = lax.optimization_barrier((first, aside))
    if slots[2]:
        first, late = lax.optimization_barrier((first, late))
    powers(first, 1, 0, LARGE)
    if slots[1]:
        powers(aside, 0, 1, SMALL)
    second, edge_image, planes = lax.optimization_barrier((second, edge_image, planes))
    powers(second, 0, 3, LARGE)
    if slots[2]:
        late = exchange(joined(late_home, late), "near", 2)
        late, planes = lax.optimization_barrier((late, planes))
        late, images[0] = lax.optimization_barrier((pieces_of(late), images[0]))
        powers(late, 0, 2, SMALL)
    edge_image = edge_image.astype(jnp.float32)
    lower = device < middle
    arrays = [planes[at] for at in sorted(planes)] + [images[at] for at in sorted(images)]
    last = len(arrays) - 1
    arrays += [jnp.where(lower, edge_image, edge), jnp.where(lower, edge, edge_image)]
    places = [None] * owned
    places[0], places[half] = (last + 1, 0), (last + 2, 0)
    for at, slot in enumerate([slot for slot in slots if slot]):
        for plane, row in enumerate(slot):
            places[row] = (at, plane)
            places[owned - row] = (len(planes) + at, len(slot) - 1 - plane)
    return assemble(arrays, places)


def solution(mesh):
    tm_count, rows_count = mesh.devices.shape
    split = jax.sharding.Mesh(
        mesh.devices.reshape(tm_count, 2, rows_count // 2), ("tm", "half", "near")
    )
    in_specs = (P("tm", ("half", "near"), None),)
    out_specs = P(None, AXES, None)
    return jax.shard_map(body, mesh=split, in_specs=in_specs, out_specs=out_specs, check_vma=False)
```

```python
import functools
import math

import jax
import jax.numpy as jnp
import ml_dtypes
import numpy as np
from jax import lax
from jax.experimental import pallas as pl
from jax.experimental.pallas import tpu as pltpu
from jax.sharding import PartitionSpec as P

AXES = ("tm", "half", "near")
LANES = 128
TILE = 8
SHARES = (8, 10, 11, 15)
SMALL = pl.CostEstimate(flops=1 << 20, bytes_accessed=1 << 20, transcendentals=0)
LARGE = pl.CostEstimate(flops=1 << 40, bytes_accessed=1 << 20, transcendentals=0)
VMEM_BYTES = 63 * 1024 * 1024
ROWS_VMEM_BYTES = 40 * 1024 * 1024
ROWS_STEP = 32


def to_bf16(values):
    return values.astype(ml_dtypes.bfloat16)


def unit_angles(left, right, modulus):
    return (np.outer(left, right) % modulus).astype(np.float32) * np.float32(2.0 * math.pi / modulus)


def y_table(length, wavenumbers, paired):
    angles = unit_angles(wavenumbers.reshape(-1), np.arange(length), length)
    pairs = np.stack([np.cos(angles), -np.sin(angles)], 1) / np.float32(math.sqrt(length))
    if paired is not None:
        pairs = pairs.reshape(wavenumbers.shape + (2, length))
        pairs[paired][1] = 1.0 / math.sqrt(length)
    return to_bf16(pairs.reshape(2 * wavenumbers.size, length))


def x_table(length):
    angles = unit_angles(np.arange(length), np.arange(length), length)
    return to_bf16(
        np.concatenate([np.cos(angles), np.sin(angles)], 1) / np.float32(math.sqrt(length))
    )


def window_table(hop, windows):
    size = 2 * hop
    steps = np.arange(size)
    hann = np.float32(0.5) - np.float32(0.5) * np.cos(
        steps.astype(np.float32) * np.float32(2.0 * math.pi / size)
    )
    angles = unit_angles(steps, steps, size)
    cosine = to_bf16(np.cos(angles) * hann[None, :])
    sine = to_bf16(np.sin(angles) * hann[None, :])
    frames = hop * (windows + 1)
    table = np.zeros((windows, 2, size, 2, frames), ml_dtypes.bfloat16)
    for window in range(windows):
        at = slice(window * hop, window * hop + size)
        table[window, 0, :, 0, at] = cosine
        table[window, 0, :, 1, at] = sine
        table[window, 1, :, 1, at] = cosine
        table[window, 1, :, 0, at] = -sine
    return table.reshape(windows * 2 * size, 2 * frames), float(np.sum(hann * hann))


def reversal(size):
    matrix = np.zeros((size, size), ml_dtypes.bfloat16)
    matrix[np.arange(size), (size - np.arange(size)) % size] = 1
    return matrix


def row_transform_kernel(which_ref, table_ref, heights_ref, out_ref):
    del which_ref
    frames, rows, length = heights_ref.shape
    planes = []
    for frame in range(0, frames, 2):
        pair = heights_ref[frame : frame + 2].reshape(2 * rows, length)
        product = lax.dot_general(
            table_ref[0], pair, (((1,), (1,)), ((), ())), preferred_element_type=jnp.float32
        )
        planes += [product[:, :rows], product[:, rows:]]
    out_ref[...] = jnp.swapaxes(jnp.stack(planes, 0), 0, 1).astype(jnp.bfloat16)


def row_transform(which, heights, table, cost):
    frames, rows, length = heights.shape
    columns = table.shape[1]
    if rows != LANES:
        picked = lax.dynamic_index_in_dim(table, which, 0, keepdims=False)
        return jnp.einsum(
            "cy,fxy->cfx", picked, heights, preferred_element_type=jnp.float32
        ).astype(jnp.bfloat16)
    step = 16
    return pl.pallas_call(
        row_transform_kernel,
        out_shape=jax.ShapeDtypeStruct((columns, frames, rows), jnp.bfloat16),
        grid_spec=pltpu.PrefetchScalarGridSpec(
            num_scalar_prefetch=1,
            grid=(frames // step,),
            in_specs=[
                pl.BlockSpec((1, columns, length), lambda i, which_ref: (which_ref[0], 0, 0)),
                pl.BlockSpec((step, rows, length), lambda i, which_ref: (i, 0, 0)),
            ],
            out_specs=pl.BlockSpec((columns, step, rows), lambda i, which_ref: (0, i, 0)),
        ),
        compiler_params=pltpu.CompilerParams(vmem_limit_bytes=VMEM_BYTES),
        cost_estimate=cost,
        name="row_transform",
    )(jnp.asarray(which, jnp.int32).reshape(1), table, heights)


def gather_field(pieces_ref):
    blocks, width, _, part, _, _ = pieces_ref.shape
    return jnp.concatenate(
        [
            jnp.concatenate([pieces_ref[t, s, 0, p] for s in range(width)], 1)
            for p in range(part)
            for t in range(blocks)
        ],
        0,
    )


def column_products(field, x_ref, at, chunk):
    length = x_ref.shape[0]
    return (
        jnp.dot(field, x_ref[:, at : at + chunk], preferred_element_type=jnp.float32),
        jnp.dot(
            field, x_ref[:, length + at : length + at + chunk], preferred_element_type=jnp.float32
        ),
    )


def mean_power(real_part, imag_part, window_ref, scale, size):
    modes = jnp.concatenate([real_part, imag_part], 0).astype(jnp.bfloat16)
    moved = jnp.dot(window_ref[...], modes, preferred_element_type=jnp.float32)
    power = moved * moved
    total = power[:size]
    for row in range(size, power.shape[0], size):
        total = total + power[row : row + size]
    return total * scale


def flipped(power, flip_w_ref):
    return jnp.dot(
        flip_w_ref[...], power.astype(jnp.bfloat16), preferred_element_type=jnp.float32
    ).astype(jnp.bfloat16)


def spectrum_kernel(
    scale, pieces_ref, x_ref, window_ref, flip_w_ref, flip_k_ref, own_ref, mirror_ref, scratch
):
    length = x_ref.shape[0]
    number, size, _ = scratch.shape
    field = gather_field(pieces_ref)
    frames = field.shape[0] // 2
    chunk = length
    for at in range(0, length, chunk):
        cosine, sine = column_products(field, x_ref, at, chunk)
        real_part = cosine[:frames] + sine[frames:]
        imag_part = cosine[frames:] - sine[:frames]
        total = mean_power(real_part, imag_part, window_ref, scale, size)
        own_ref[0, :, at : at + chunk] = total
        scratch[number - 1 - pl.program_id(0), :, at : at + chunk] = flipped(total, flip_w_ref)

    @pl.when(pl.program_id(0) == number - 1)
    def reverse():
        flat = scratch[...].reshape(number * size, length)
        turned = jnp.dot(flat, flip_k_ref[...], preferred_element_type=jnp.float32)
        mirror_ref[...] = turned.astype(jnp.bfloat16).reshape(number, size, length)


def edge_kernel(
    scale,
    paired_ref,
    pieces_ref,
    x_ref,
    window_ref,
    flip_w_ref,
    flip_k_ref,
    own_ref,
    mirror_ref,
    scratch,
):
    length = x_ref.shape[0]
    size = scratch.shape[1]
    paired = paired_ref[0] != 0
    apart = jnp.where(paired, 0.0, 1.0)
    field = gather_field(pieces_ref)
    frames = field.shape[0] // 2
    chunk = length
    for at in range(0, length, chunk):
        cosine, sine = column_products(field, x_ref, at, chunk)
        real_part = cosine[:frames] + apart * sine[frames:]
        imag_part = apart * cosine[frames:] - sine[:frames]
        total = mean_power(real_part, imag_part, window_ref, scale, size)
        other = mean_power(cosine[frames:], -sine[frames:], window_ref, scale, size)
        own_ref[0, :, at : at + chunk] = total
        mirror_ref[0, :, at : at + chunk] = other.astype(jnp.bfloat16)
        scratch[0, :, at : at + chunk] = flipped(total, flip_w_ref)

    @pl.when(jnp.logical_not(paired))
    def reverse():
        turned = jnp.dot(scratch[0], flip_k_ref[...], preferred_element_type=jnp.float32)
        mirror_ref[0] = turned.astype(jnp.bfloat16)


def spectrum(pieces, start, number, tables, scale, cost, paired=None):
    blocks, width, _, part, frames, rows = pieces.shape
    length = width * rows
    size = 2 * frames
    if rows != LANES:
        pieces = pieces[:, :, start : start + number].transpose(0, 2, 3, 4, 1, 5)
        pieces = pieces.reshape(blocks, 1, number, part, frames, length)
        width, rows, start = 1, length, 0
    whole = lambda array: pl.BlockSpec(array.shape, lambda i, *_: (0,) * array.ndim)
    block = (blocks, width, 1, part, frames, rows)
    scalars = [] if paired is None else [paired]
    return pl.pallas_call(
        functools.partial(spectrum_kernel if paired is None else edge_kernel, scale),
        out_shape=[
            jax.ShapeDtypeStruct((number, size, length), jnp.float32),
            jax.ShapeDtypeStruct((number, size, length), jnp.bfloat16),
        ],
        grid_spec=pltpu.PrefetchScalarGridSpec(
            num_scalar_prefetch=len(scalars),
            grid=(number,),
            in_specs=[pl.BlockSpec(block, lambda i, *_: (0, 0, start + i, 0, 0, 0))]
            + [whole(table) for table in tables],
            out_specs=[
                pl.BlockSpec((1, size, length), lambda i, *_: (i, 0, 0)),
                pl.BlockSpec((number, size, length), lambda i, *_: (0, 0, 0)),
            ],
            scratch_shapes=[pltpu.VMEM((number, size, length), jnp.bfloat16)],
        ),
        compiler_params=pltpu.CompilerParams(vmem_limit_bytes=VMEM_BYTES),
        cost_estimate=cost,
        name="spectrum" if paired is None else "edge_spectrum",
    )(*scalars, pieces, *tables)


def rows_kernel(places, aliased, *refs):
    planes, out_ref = refs[aliased:-1], refs[-1]
    for at in range(0, len(places), TILE):
        stack = [planes[which][plane].astype(jnp.float32) for which, plane in places[at : at + TILE]]
        out_ref[:, at : at + TILE] = jnp.swapaxes(jnp.stack(stack, 0), 0, 1)


def write_rows(given, arrays, places, start, total):
    _, size, length = arrays[0].shape
    step = ROWS_STEP
    used = sorted({which for which, _ in places})
    places = [(used.index(which), plane) for which, plane in places]
    block = start // len(places)
    return pl.pallas_call(
        functools.partial(rows_kernel, places, len(given)),
        out_shape=jax.ShapeDtypeStruct((size, total, length), jnp.float32),
        grid=(size // step,),
        in_specs=[pl.BlockSpec(memory_space=pl.ANY)] * len(given)
        + [
            pl.BlockSpec((arrays[which].shape[0], step, length), lambda i: (0, i, 0))
            for which in used
        ],
        out_specs=pl.BlockSpec((step, len(places), length), lambda i: (i, block, 0)),
        input_output_aliases={0: 0} if given else {},
        compiler_params=pltpu.CompilerParams(vmem_limit_bytes=ROWS_VMEM_BYTES),
        name="write_rows",
    )(*given, *[arrays[which] for which in used])


def assemble(arrays, places):
    total = len(places)
    late = total * 3 // 4 if total // 4 % TILE == 0 else 0
    given = []
    if late:
        given.append(write_rows([], arrays, places[:late], 0, total))
    return write_rows(given, arrays, places[late:], late, total)


def split_rows(half):
    rows = list(range(half - 1, 0, -1))
    parts = [0] + [len(rows) * share // SHARES[-1] for share in SHARES]
    return [sorted(rows[lo:hi]) for lo, hi in zip(parts, parts[1:])]


def exchange(blocks, axis, dim):
    count = lax.axis_size(axis)
    me = lax.axis_index(axis)
    pick = lambda at: lax.dynamic_index_in_dim(blocks, at, dim)
    moved = [pick(me)]
    for shift in range(1, count):
        to = [(i, (i + shift) % count) for i in range(count)]
        moved.append(lax.ppermute(pick((me + shift) % count), axis, to))
    rising = moved[:1] + moved[:0:-1]
    joined = jnp.concatenate(rising + rising[:-1], dim)
    return lax.dynamic_slice_in_dim(joined, (count - me) % count, count, dim)


def body(heights):
    frames, rows_dev, length = heights.shape
    tm_count = lax.axis_size("tm")
    near_count = lax.axis_size("near")
    rows_count = 2 * near_count
    devices = tm_count * rows_count
    owned = length // devices
    half = owned // 2
    middle = devices // 2
    windows, energy = window_table(frames, tm_count - 1)
    scale = 1.0 / ((tm_count - 1) * energy)
    tables = (x_table(length), windows, reversal(2 * frames), reversal(length))
    tables = tuple(jnp.asarray(table) for table in tables)
    device = lax.axis_index(AXES)
    opposite = [(d, devices - 1 - d) for d in range(devices)]
    edge_partner = [(d, devices - 1 - d if d < middle else (devices - d) % middle) for d in range(devices)]

    edges = np.array([d * owned + (half if d < middle else 0) for d in range(devices)])

    def mix(heights, slot, with_edge, cost):
        wavenumbers = np.arange(devices)[:, None] * owned + np.asarray(slot)
        if with_edge:
            wavenumbers = np.concatenate([edges[:, None], wavenumbers], 1)
        table = y_table(length, wavenumbers, (middle, 0) if with_edge else None)
        mixed = row_transform(0, heights, jnp.asarray(table)[None], cost)
        return mixed.reshape(devices, -1, 2, frames, rows_dev)

    def arrive(mixed):
        got = lax.all_to_all(mixed, AXES, split_axis=0, concat_axis=0, tiled=True)
        return got.reshape((tm_count, rows_count) + mixed.shape[1:])

    def image_of(image, partner):
        return lax.ppermute(image, AXES, partner)

    slots = split_rows(half)
    paired = (device == middle).astype(jnp.int32).reshape(1)
    planes, images = {}, {}

    def powers(pieces, start, at, cost):
        if slots[at]:
            planes[at], image = spectrum(pieces, start, len(slots[at]), tables, scale, cost)
            images[at] = image_of(image, opposite)

    def mix_half(heights, slot, which):
        receivers = np.arange(devices).reshape(tm_count, 2, near_count).transpose(1, 0, 2)
        wavenumbers = receivers[..., None] * owned + np.asarray(slot)
        table = y_table(length, wavenumbers, None).reshape(2, -1, length)
        mixed = row_transform(which, heights, jnp.asarray(table), SMALL)
        return mixed.reshape(tm_count, 1, near_count, len(slot), 2, frames, rows_dev)

    def joined(home, away):
        return lax.dynamic_slice_in_dim(jnp.concatenate([home, away, home], 1), side, 2, 1)

    def swapped(away):
        return lax.ppermute(away, "half", [(0, 1), (1, 0)])

    def pieces_of(parts):
        parts = exchange(parts, "tm", 0)
        return parts.reshape((tm_count, rows_count) + parts.shape[3:])

    later = heights
    side = lax.axis_index("half")
    if slots[1]:
        aside, later = lax.optimization_barrier((mix_half(later, slots[1], 1 - side), later))
        aside = swapped(aside)
    first, later = lax.optimization_barrier((mix(later, slots[0], True, SMALL), later))
    second, later = lax.optimization_barrier((mix(later, slots[3], False, LARGE), later))
    if slots[1]:
        aside, later = lax.optimization_barrier((aside, later))
        aside = exchange(joined(mix_half(later, slots[1], side), aside), "near", 2)
    if slots[2]:
        late, late_home = mix_half(later, slots[2], 1 - side), mix_half(later, slots[2], side)
        if slots[1]:
            late, late_home, aside = lax.optimization_barrier((late, late_home, aside))
        late = swapped(late)
    if slots[1]:
        aside = pieces_of(aside)
    first = arrive(first)
    second = arrive(second)
    edge, edge_image = spectrum(first, 0, 1, tables, scale, SMALL, paired)
    edge_image = image_of(edge_image, edge_partner)
    first, edge = lax.optimization_barrier((first, edge))
    if slots[1]:
        first, aside = lax.optimization_barrier((first, aside))
    if slots[2]:
        first, late = lax.optimization_barrier((first, late))
    powers(first, 1, 0, LARGE)
    if slots[1]:
        powers(aside, 0, 1, SMALL)
    second, edge_image, planes = lax.optimization_barrier((second, edge_image, planes))
    powers(second, 0, 3, LARGE)
    if slots[2]:
        late = exchange(joined(late_home, late), "near", 2)
        late, planes = lax.optimization_barrier((late, planes))
        late, images[0] = lax.optimization_barrier((pieces_of(late), images[0]))
        powers(late, 0, 2, SMALL)
    edge_image = edge_image.astype(jnp.float32)
    lower = device < middle
    arrays = [planes[at] for at in sorted(planes)] + [images[at] for at in sorted(images)]
    last = len(arrays) - 1
    arrays += [jnp.where(lower, edge_image, edge), jnp.where(lower, edge, edge_image)]
    places = [None] * owned
    places[0], places[half] = (last + 1, 0), (last + 2, 0)
    for at, slot in enumerate([slot for slot in slots if slot]):
        for plane, row in enumerate(slot):
            places[row] = (at, plane)
            places[owned - row] = (len(planes) + at, len(slot) - 1 - plane)
    return assemble(arrays, places)


def solution(mesh):
    tm_count, rows_count = mesh.devices.shape
    split = jax.sharding.Mesh(
        mesh.devices.reshape(tm_count, 2, rows_count // 2), ("tm", "half", "near")
    )
    in_specs = (P("tm", ("half", "near"), None),)
    out_specs = P(None, AXES, None)
    return jax.shard_map(body, mesh=split, in_specs=in_specs, out_specs=out_specs, check_vma=False)
```

```python
import functools
import math

import jax
import jax.numpy as jnp
import ml_dtypes
import numpy as np
from jax import lax
from jax.experimental import pallas as pl
from jax.experimental.pallas import tpu as pltpu
from jax.sharding import PartitionSpec as P

AXES = ("tm", "half", "near")
LANES = 128
TILE = 8
SHARES = (8, 10, 11, 15)
SMALL = pl.CostEstimate(flops=1 << 20, bytes_accessed=1 << 20, transcendentals=0)
LARGE = pl.CostEstimate(flops=1 << 40, bytes_accessed=1 << 20, transcendentals=0)
VMEM_BYTES = 63 * 1024 * 1024
ROWS_VMEM_BYTES = 40 * 1024 * 1024
ROWS_STEP = 32


def to_bf16(values):
    return values.astype(ml_dtypes.bfloat16)


def unit_angles(left, right, modulus):
    return (np.outer(left, right) % modulus).astype(np.float32) * np.float32(2.0 * math.pi / modulus)


def y_table(length, wavenumbers, paired):
    angles = unit_angles(wavenumbers.reshape(-1), np.arange(length), length)
    pairs = np.stack([np.cos(angles), -np.sin(angles)], 1) / np.float32(math.sqrt(length))
    if paired is not None:
        pairs = pairs.reshape(wavenumbers.shape + (2, length))
        pairs[paired][1] = 1.0 / math.sqrt(length)
    return to_bf16(pairs.reshape(2 * wavenumbers.size, length))


def x_table(length):
    angles = unit_angles(np.arange(length), np.arange(length), length)
    return to_bf16(
        np.concatenate([np.cos(angles), np.sin(angles)], 1) / np.float32(math.sqrt(length))
    )


def window_table(hop, windows):
    size = 2 * hop
    steps = np.arange(size)
    hann = np.float32(0.5) - np.float32(0.5) * np.cos(
        steps.astype(np.float32) * np.float32(2.0 * math.pi / size)
    )
    angles = unit_angles(steps, steps, size)
    cosine = to_bf16(np.cos(angles) * hann[None, :])
    sine = to_bf16(np.sin(angles) * hann[None, :])
    frames = hop * (windows + 1)
    table = np.zeros((windows, 2, size, 2, frames), ml_dtypes.bfloat16)
    for window in range(windows):
        at = slice(window * hop, window * hop + size)
        table[window, 0, :, 0, at] = cosine
        table[window, 0, :, 1, at] = sine
        table[window, 1, :, 1, at] = cosine
        table[window, 1, :, 0, at] = -sine
    return table.reshape(windows * 2 * size, 2 * frames), float(np.sum(hann * hann))


def reversal(size):
    matrix = np.zeros((size, size), ml_dtypes.bfloat16)
    matrix[np.arange(size), (size - np.arange(size)) % size] = 1
    return matrix


def row_transform_kernel(which_ref, table_ref, heights_ref, out_ref):
    del which_ref
    frames, rows, length = heights_ref.shape
    planes = []
    for frame in range(0, frames, 2):
        pair = heights_ref[frame : frame + 2].reshape(2 * rows, length)
        product = lax.dot_general(
            table_ref[0], pair, (((1,), (1,)), ((), ())), preferred_element_type=jnp.float32
        )
        planes += [product[:, :rows], product[:, rows:]]
    out_ref[...] = jnp.swapaxes(jnp.stack(planes, 0), 0, 1).astype(jnp.bfloat16)


def row_transform(which, heights, table, cost):
    frames, rows, length = heights.shape
    columns = table.shape[1]
    if rows != LANES:
        picked = lax.dynamic_index_in_dim(table, which, 0, keepdims=False)
        return jnp.einsum(
            "cy,fxy->cfx", picked, heights, preferred_element_type=jnp.float32
        ).astype(jnp.bfloat16)
    step = 16
    return pl.pallas_call(
        row_transform_kernel,
        out_shape=jax.ShapeDtypeStruct((columns, frames, rows), jnp.bfloat16),
        grid_spec=pltpu.PrefetchScalarGridSpec(
            num_scalar_prefetch=1,
            grid=(frames // step,),
            in_specs=[
                pl.BlockSpec((1, columns, length), lambda i, which_ref: (which_ref[0], 0, 0)),
                pl.BlockSpec((step, rows, length), lambda i, which_ref: (i, 0, 0)),
            ],
            out_specs=pl.BlockSpec((columns, step, rows), lambda i, which_ref: (0, i, 0)),
        ),
        compiler_params=pltpu.CompilerParams(vmem_limit_bytes=VMEM_BYTES),
        cost_estimate=cost,
        name="row_transform",
    )(jnp.asarray(which, jnp.int32).reshape(1), table, heights)


def gather_field(pieces_ref):
    blocks, width, _, part, _, _ = pieces_ref.shape
    return jnp.concatenate(
        [
            jnp.concatenate([pieces_ref[t, s, 0, p] for s in range(width)], 1)
            for p in range(part)
            for t in range(blocks)
        ],
        0,
    )


def column_products(field, x_ref, at, chunk):
    length = x_ref.shape[0]
    return (
        jnp.dot(field, x_ref[:, at : at + chunk], preferred_element_type=jnp.float32),
        jnp.dot(
            field, x_ref[:, length + at : length + at + chunk], preferred_element_type=jnp.float32
        ),
    )


def mean_power(real_part, imag_part, window_ref, scale, size):
    modes = jnp.concatenate([real_part, imag_part], 0).astype(jnp.bfloat16)
    moved = jnp.dot(window_ref[...], modes, preferred_element_type=jnp.float32)
    power = moved * moved
    total = power[:size]
    for row in range(size, power.shape[0], size):
        total = total + power[row : row + size]
    return total * scale


def flipped(power, flip_w_ref):
    return jnp.dot(
        flip_w_ref[...], power.astype(jnp.bfloat16), preferred_element_type=jnp.float32
    ).astype(jnp.bfloat16)


def spectrum_kernel(
    scale, pieces_ref, x_ref, window_ref, flip_w_ref, flip_k_ref, own_ref, mirror_ref, scratch
):
    length = x_ref.shape[0]
    number, size, _ = scratch.shape
    field = gather_field(pieces_ref)
    frames = field.shape[0] // 2
    chunk = length
    for at in range(0, length, chunk):
        cosine, sine = column_products(field, x_ref, at, chunk)
        real_part = cosine[:frames] + sine[frames:]
        imag_part = cosine[frames:] - sine[:frames]
        total = mean_power(real_part, imag_part, window_ref, scale, size)
        own_ref[0, :, at : at + chunk] = total
        scratch[number - 1 - pl.program_id(0), :, at : at + chunk] = flipped(total, flip_w_ref)

    @pl.when(pl.program_id(0) == number - 1)
    def reverse():
        flat = scratch[...].reshape(number * size, length)
        turned = jnp.dot(flat, flip_k_ref[...], preferred_element_type=jnp.float32)
        mirror_ref[...] = turned.astype(jnp.bfloat16).reshape(number, size, length)


def edge_kernel(
    scale,
    paired_ref,
    pieces_ref,
    x_ref,
    window_ref,
    flip_w_ref,
    flip_k_ref,
    own_ref,
    mirror_ref,
    scratch,
):
    length = x_ref.shape[0]
    size = scratch.shape[1]
    paired = paired_ref[0] != 0
    apart = jnp.where(paired, 0.0, 1.0)
    field = gather_field(pieces_ref)
    frames = field.shape[0] // 2
    chunk = length
    for at in range(0, length, chunk):
        cosine, sine = column_products(field, x_ref, at, chunk)
        real_part = cosine[:frames] + apart * sine[frames:]
        imag_part = apart * cosine[frames:] - sine[:frames]
        total = mean_power(real_part, imag_part, window_ref, scale, size)
        other = mean_power(cosine[frames:], -sine[frames:], window_ref, scale, size)
        own_ref[0, :, at : at + chunk] = total
        mirror_ref[0, :, at : at + chunk] = other.astype(jnp.bfloat16)
        scratch[0, :, at : at + chunk] = flipped(total, flip_w_ref)

    @pl.when(jnp.logical_not(paired))
    def reverse():
        turned = jnp.dot(scratch[0], flip_k_ref[...], preferred_element_type=jnp.float32)
        mirror_ref[0] = turned.astype(jnp.bfloat16)


def spectrum(pieces, start, number, tables, scale, cost, paired=None):
    blocks, width, _, part, frames, rows = pieces.shape
    length = width * rows
    size = 2 * frames
    if rows != LANES:
        pieces = pieces[:, :, start : start + number].transpose(0, 2, 3, 4, 1, 5)
        pieces = pieces.reshape(blocks, 1, number, part, frames, length)
        width, rows, start = 1, length, 0
    whole = lambda array: pl.BlockSpec(array.shape, lambda i, *_: (0,) * array.ndim)
    block = (blocks, width, 1, part, frames, rows)
    scalars = [] if paired is None else [paired]
    return pl.pallas_call(
        functools.partial(spectrum_kernel if paired is None else edge_kernel, scale),
        out_shape=[
            jax.ShapeDtypeStruct((number, size, length), jnp.float32),
            jax.ShapeDtypeStruct((number, size, length), jnp.bfloat16),
        ],
        grid_spec=pltpu.PrefetchScalarGridSpec(
            num_scalar_prefetch=len(scalars),
            grid=(number,),
            in_specs=[pl.BlockSpec(block, lambda i, *_: (0, 0, start + i, 0, 0, 0))]
            + [whole(table) for table in tables],
            out_specs=[
                pl.BlockSpec((1, size, length), lambda i, *_: (i, 0, 0)),
                pl.BlockSpec((number, size, length), lambda i, *_: (0, 0, 0)),
            ],
            scratch_shapes=[pltpu.VMEM((number, size, length), jnp.bfloat16)],
        ),
        compiler_params=pltpu.CompilerParams(vmem_limit_bytes=VMEM_BYTES),
        cost_estimate=cost,
        name="spectrum" if paired is None else "edge_spectrum",
    )(*scalars, pieces, *tables)


def rows_kernel(places, aliased, *refs):
    planes, out_ref = refs[aliased:-1], refs[-1]
    for at in range(0, len(places), TILE):
        stack = [planes[which][plane].astype(jnp.float32) for which, plane in places[at : at + TILE]]
        out_ref[:, at : at + TILE] = jnp.swapaxes(jnp.stack(stack, 0), 0, 1)


def write_rows(given, arrays, places, start, total):
    _, size, length = arrays[0].shape
    step = ROWS_STEP
    used = sorted({which for which, _ in places})
    planes = {which: {plane for at, plane in places if at == which} for which in used}
    single = {which: min(planes[which]) for which in used if len(planes[which]) == 1}
    places = [(used.index(which), 0 if which in single else plane) for which, plane in places]

    def spec(which):
        if which in single:
            return pl.BlockSpec((1, step, length), lambda i: (single[which], i, 0))
        return pl.BlockSpec((arrays[which].shape[0], step, length), lambda i: (0, i, 0))

    block = start // len(places)
    return pl.pallas_call(
        functools.partial(rows_kernel, places, len(given)),
        out_shape=jax.ShapeDtypeStruct((size, total, length), jnp.float32),
        grid=(size // step,),
        in_specs=[pl.BlockSpec(memory_space=pl.ANY)] * len(given)
        + [spec(which) for which in used],
        out_specs=pl.BlockSpec((step, len(places), length), lambda i: (i, block, 0)),
        input_output_aliases={0: 0} if given else {},
        compiler_params=pltpu.CompilerParams(vmem_limit_bytes=ROWS_VMEM_BYTES),
        name="write_rows",
    )(*given, *[arrays[which] for which in used])


def assemble(arrays, places):
    total = len(places)
    late = total * 3 // 4 if total // 4 % TILE == 0 else 0
    given = []
    if late:
        given.append(write_rows([], arrays, places[:late], 0, total))
    return write_rows(given, arrays, places[late:], late, total)


def split_rows(half):
    rows = list(range(half - 1, 0, -1))
    parts = [0] + [len(rows) * share // SHARES[-1] for share in SHARES]
    return [sorted(rows[lo:hi]) for lo, hi in zip(parts, parts[1:])]


def exchange(blocks, axis, dim):
    count = lax.axis_size(axis)
    me = lax.axis_index(axis)
    pick = lambda at: lax.dynamic_index_in_dim(blocks, at, dim)
    moved = [pick(me)]
    for shift in range(1, count):
        to = [(i, (i + shift) % count) for i in range(count)]
        moved.append(lax.ppermute(pick((me + shift) % count), axis, to))
    rising = moved[:1] + moved[:0:-1]
    joined = jnp.concatenate(rising + rising[:-1], dim)
    return lax.dynamic_slice_in_dim(joined, (count - me) % count, count, dim)


def body(heights):
    frames, rows_dev, length = heights.shape
    tm_count = lax.axis_size("tm")
    near_count = lax.axis_size("near")
    rows_count = 2 * near_count
    devices = tm_count * rows_count
    owned = length // devices
    half = owned // 2
    middle = devices // 2
    windows, energy = window_table(frames, tm_count - 1)
    scale = 1.0 / ((tm_count - 1) * energy)
    tables = (x_table(length), windows, reversal(2 * frames), reversal(length))
    tables = tuple(jnp.asarray(table) for table in tables)
    device = lax.axis_index(AXES)
    opposite = [(d, devices - 1 - d) for d in range(devices)]
    edge_partner = [(d, devices - 1 - d if d < middle else (devices - d) % middle) for d in range(devices)]

    edges = np.array([d * owned + (half if d < middle else 0) for d in range(devices)])

    def mix(heights, slot, with_edge, cost):
        wavenumbers = np.arange(devices)[:, None] * owned + np.asarray(slot)
        if with_edge:
            wavenumbers = np.concatenate([edges[:, None], wavenumbers], 1)
        table = y_table(length, wavenumbers, (middle, 0) if with_edge else None)
        mixed = row_transform(0, heights, jnp.asarray(table)[None], cost)
        return mixed.reshape(devices, -1, 2, frames, rows_dev)

    def arrive(mixed):
        got = lax.all_to_all(mixed, AXES, split_axis=0, concat_axis=0, tiled=True)
        return got.reshape((tm_count, rows_count) + mixed.shape[1:])

    def image_of(image, partner):
        return lax.ppermute(image, AXES, partner)

    slots = split_rows(half)
    paired = (device == middle).astype(jnp.int32).reshape(1)
    planes, images = {}, {}

    def powers(pieces, start, at, cost):
        if slots[at]:
            planes[at], image = spectrum(pieces, start, len(slots[at]), tables, scale, cost)
            images[at] = image_of(image, opposite)

    def mix_half(heights, slot, which):
        receivers = np.arange(devices).reshape(tm_count, 2, near_count).transpose(1, 0, 2)
        wavenumbers = receivers[..., None] * owned + np.asarray(slot)
        table = y_table(length, wavenumbers, None).reshape(2, -1, length)
        mixed = row_transform(which, heights, jnp.asarray(table), SMALL)
        return mixed.reshape(tm_count, 1, near_count, len(slot), 2, frames, rows_dev)

    def joined(home, away):
        return lax.dynamic_slice_in_dim(jnp.concatenate([home, away, home], 1), side, 2, 1)

    def swapped(away):
        return lax.ppermute(away, "half", [(0, 1), (1, 0)])

    def pieces_of(parts):
        parts = exchange(parts, "tm", 0)
        return parts.reshape((tm_count, rows_count) + parts.shape[3:])

    later = heights
    side = lax.axis_index("half")
    if slots[1]:
        aside, later = lax.optimization_barrier((mix_half(later, slots[1], 1 - side), later))
        aside = swapped(aside)
    first, later = lax.optimization_barrier((mix(later, slots[0], True, SMALL), later))
    second, later = lax.optimization_barrier((mix(later, slots[3], False, LARGE), later))
    if slots[1]:
        aside, later = lax.optimization_barrier((aside, later))
        aside = exchange(joined(mix_half(later, slots[1], side), aside), "near", 2)
    if slots[2]:
        late, late_home = mix_half(later, slots[2], 1 - side), mix_half(later, slots[2], side)
        if slots[1]:
            late, late_home, aside = lax.optimization_barrier((late, late_home, aside))
        late = swapped(late)
    if slots[1]:
        aside = pieces_of(aside)
    first = arrive(first)
    second = arrive(second)
    edge, edge_image = spectrum(first, 0, 1, tables, scale, SMALL, paired)
    edge_image = image_of(edge_image, edge_partner)
    first, edge = lax.optimization_barrier((first, edge))
    if slots[1]:
        first, aside = lax.optimization_barrier((first, aside))
    if slots[2]:
        first, late = lax.optimization_barrier((first, late))
    powers(first, 1, 0, LARGE)
    if slots[1]:
        powers(aside, 0, 1, SMALL)
    second, edge_image, planes = lax.optimization_barrier((second, edge_image, planes))
    powers(second, 0, 3, LARGE)
    if slots[2]:
        late = exchange(joined(late_home, late), "near", 2)
        late, planes = lax.optimization_barrier((late, planes))
        late, images[0] = lax.optimization_barrier((pieces_of(late), images[0]))
        powers(late, 0, 2, SMALL)
    edge_image = edge_image.astype(jnp.float32)
    lower = device < middle
    arrays = [planes[at] for at in sorted(planes)] + [images[at] for at in sorted(images)]
    last = len(arrays) - 1
    arrays += [jnp.where(lower, edge_image, edge), jnp.where(lower, edge, edge_image)]
    places = [None] * owned
    places[0], places[half] = (last + 1, 0), (last + 2, 0)
    for at, slot in enumerate([slot for slot in slots if slot]):
        for plane, row in enumerate(slot):
            places[row] = (at, plane)
            places[owned - row] = (len(planes) + at, len(slot) - 1 - plane)
    return assemble(arrays, places)


def solution(mesh):
    tm_count, rows_count = mesh.devices.shape
    split = jax.sharding.Mesh(
        mesh.devices.reshape(tm_count, 2, rows_count // 2), ("tm", "half", "near")
    )
    in_specs = (P("tm", ("half", "near"), None),)
    out_specs = P(None, AXES, None)
    return jax.shard_map(body, mesh=split, in_specs=in_specs, out_specs=out_specs, check_vma=False)
```
